128 devices in a mesh: oct: 8 (over x, core), leaf: 16 (over z, y).
Axes of the slice: x: 4, y: 4, z: 4, core: 2. Of those that a mesh axis runs over, the one named last changes fastest.
Arguments:
- density: float32 [65536, 128], P(('oct', 'leaf')), may hold values from -6 to 6
- positions: float32 [65536, 3, 128], P(('oct', 'leaf')), may hold values from -1 to 1
- counts: int32 [65536], P(('oct', 'leaf')), may hold values from 1 to 128, as said below
- leaf_parent: int32 [65536], P(('oct', 'leaf')), may hold values from 0 to 63
- child_pos: int32 [65536], P(('oct', 'leaf')), may hold values from 0 to 7
- send_slots: int32 [128, 128, 32], P(('oct', 'leaf')), may hold values from -1 to 511, as said below
- far_source: int32 [65536, 27], P(('oct', 'leaf')), may hold values from 0 to 4095, as said below
- far_type: int32 [65536, 27], P(('oct', 'leaf')), may hold values from 0 to 63
- near_offset: int32 [65536, 4], P(('oct', 'leaf')), may hold values from -32 to 32, as said below
- near_dir: int32 [65536, 4], P(('oct', 'leaf')), may hold values from 0 to 26
- coarse_source: int32 [512, 16], P('oct'), may hold values from 0 to 511
- coarse_type: int32 [512, 16], P('oct'), may hold values from 0 to 63
- m2l: bfloat16 [64, 256, 256], replicated, may hold values from -0.375 to 0.375
- m2m: bfloat16 [8, 256, 256], replicated, may hold values from -0.03125 to 0.03125
- l2l: bfloat16 [8, 256, 256], replicated, may hold values from -0.375 to 0.375
Outputs:
- potential: float32 [65536, 128], P(('oct', 'leaf'))
The draws below stay inside these ranges and needn't reach their ends.
Inputs may be any that keep to these rules, and one draw needn't show every extreme that they name: `counts`: each device's first leaf holds 128 panels; the lightest leaves of a device differ from device to device. `send_slots`: entry [o, d, s] is a leaf of device o, counted within its block, sent to device d in slot s, or -1 for an empty slot. Only partner devices exchange: those of one octant group whose leaf indices differ by at most 2, and those with the same leaf index in the adjacent octant groups or in the octant group halfway round (cyclically); such a pair fills its first 16 to 32 slots, all other pairs none, and every device fills all 32 slots to some one device. `far_source`: each entry o * 32 + s names a filled slot s that device o sends to the device owning the leaf; o is that device or one of its partners. `near_offset`: the neighbour lies in the same octant group; the first entry is the leaf itself (0).
All inputs are finite; a program needn't handle non-finite values.
Results may differ from the reference program's by a relative error of at most 0.012.
Values may be sent and summed in bfloat16 or wider, within the bound.
No kernel may reach another device: no remote copies, remote signals or barrier semaphores. Data moves between devices by JAX's collectives and lax.ppermute only.
A program may use at most 128 MiB of HBM per device.

```python
import math
import jax
import jax.numpy as jnp
from jax import lax

K = 256
PAN = 128
LEAF_DEV = 512
NT = 64
NL = 27
NB = 4
CAP = 32
HW = 32
PAR = 64
NC = 16
LEAVES = 65536
GROUP_LEAVES = 8192
CHILDREN = 128
TOP = 512
N_OCT = 8
N_LEAF = 16
DEVICES = 128


def neighbour_of(device, which):
    group = device // N_LEAF
    place = device % N_LEAF
    inside = group * N_LEAF + jnp.clip(place + which - 2, 0, N_LEAF - 1)
    upper = (group + 1) % N_OCT * N_LEAF + place
    lower = (group + N_OCT - 1) % N_OCT * N_LEAF + place
    opposite = (group + N_OCT // 2) % N_OCT * N_LEAF + place
    return jnp.where(which < 5, inside, jnp.where(which == 5, upper, jnp.where(which == 6, lower, opposite))).astype(jnp.int32)


def near_table():
    device = jnp.arange(DEVICES, dtype=jnp.int32)
    group = device // N_LEAF
    place = device % N_LEAF
    same_group = (group[:, None] == group[None, :]) & (jnp.abs(place[:, None] - place[None, :]) <= 2)
    step_up = (group[:, None] - group[None, :] + N_OCT) % N_OCT
    across = (place[:, None] == place[None, :]) & ((step_up == 1) | (step_up == N_OCT - 1) | (step_up == N_OCT // 2))
    return same_group | across


def fetch_counts(key):
    first_key = jax.random.fold_in(key, 11)
    second_key = jax.random.fold_in(key, 12)
    filled = jax.random.randint(first_key, (DEVICES, DEVICES), CAP // 2, CAP + 1, dtype=jnp.int32)
    filled = jnp.where(near_table(), filled, 0)
    device = jnp.arange(DEVICES, dtype=jnp.int32)
    partner = neighbour_of(device, jax.random.randint(second_key, (DEVICES,), 0, 8, dtype=jnp.int32))
    return filled.at[device, partner].set(CAP)


def placed_panels(key, period):
    value_key, pick_key = jax.random.split(key)
    spread_values = jax.random.uniform(value_key, (LEAVES, 3, PAN), jnp.float32, -1.0, 1.0)
    picked = jax.random.randint(pick_key, (LEAVES,), 0, period, dtype=jnp.int32) == 0
    corner_values = jnp.where(spread_values < 0.0, -1.0, 1.0) * (0.8 + 0.2 * jnp.abs(spread_values))
    return jnp.where(picked[:, None, None], corner_values, spread_values).astype(jnp.float32)


def draw_positions(key, part):
    key = jax.random.fold_in(key, 13)
    return placed_panels(key, 4)


def draw_counts(key, part):
    key = jax.random.fold_in(key, 7)
    first_key, second_key = jax.random.split(key)
    lightest = jax.random.randint(first_key, (DEVICES,), PAN // 8, PAN // 2 + 1, dtype=jnp.int32)
    raw_values = jax.random.randint(second_key, (LEAVES,), 0, PAN + 1, dtype=jnp.int32)
    floors = jnp.repeat(lightest, LEAF_DEV)
    values = floors + raw_values % (PAN + 1 - floors)
    leading = jnp.arange(LEAVES, dtype=jnp.int32) % LEAF_DEV == 0
    return jnp.where(leading, PAN, values).astype(jnp.int32)


def draw_send_slots(key, part):
    filled = fetch_counts(key)
    key = jax.random.fold_in(key, 3)
    chosen = jax.random.randint(key, (DEVICES, DEVICES, CAP), 0, LEAF_DEV, dtype=jnp.int32)
    used = jnp.arange(CAP, dtype=jnp.int32)[None, None, :] < filled[:, :, None]
    return jnp.where(used, chosen, -1).astype(jnp.int32)


def draw_far_source(key, part):
    filled = fetch_counts(key)
    key = jax.random.fold_in(key, 5)
    owner_key, slot_key = jax.random.split(key)
    holder = (jnp.arange(LEAVES, dtype=jnp.int32) // LEAF_DEV)[:, None]
    which = jax.random.randint(owner_key, (LEAVES, NL), 0, 8, dtype=jnp.int32)
    owners = neighbour_of(jnp.broadcast_to(holder, (LEAVES, NL)), which)
    raw_values = jax.random.randint(slot_key, (LEAVES, NL), 0, 1 << 20, dtype=jnp.int32)
    slots = raw_values % jnp.maximum(filled[owners, holder], 1)
    return (owners * CAP + slots).astype(jnp.int32)


def draw_near_offset(key, part):
    key = jax.random.fold_in(key, 9)
    leaf_index = jnp.arange(LEAVES, dtype=jnp.int32)[:, None]
    group_start = leaf_index // GROUP_LEAVES * GROUP_LEAVES
    jump_sizes = jax.random.randint(key, (LEAVES, NB), -HW, HW + 1, dtype=jnp.int32)
    target = jnp.clip(leaf_index + jump_sizes, group_start, group_start + GROUP_LEAVES - 1)
    offsets = target - leaf_index
    return offsets.at[:, 0].set(0).astype(jnp.int32)


def touch_ends(array, key, least, top_value):
    longest = array.shape.index(max(array.shape))
    spots = []
    for shift in (0, 1):
        where = [jax.random.randint(jax.random.fold_in(key, axis), (), 0, length) for axis, length in enumerate(array.shape)]
        where[longest] = (where[longest] + shift) % array.shape[longest]
        spots.append(tuple(where))
    return array.at[spots[0]].set(least).at[spots[1]].set(top_value)


def levels(rng, extent, cuts, least, high):
    level, own = 1.0, jax.random.fold_in(rng, 6)
    for axis_at, blocks in cuts:
        draws = jnp.exp(jax.random.uniform(jax.random.fold_in(own, axis_at), (blocks,), jnp.float32, least / len(cuts), high / len(cuts)))
        level = level * jnp.repeat(draws, extent[axis_at] // blocks).reshape([-1 if axis == axis_at else 1 for axis in range(len(extent))])
    return level


def gaussian(stream_key, dims, scale, most, cuts=(), kind=jnp.bfloat16):
    values = jax.random.normal(stream_key, dims, jnp.float32) * scale
    if len(cuts) > 0:
        values = levels(stream_key, dims, cuts, -0.22, 0.18) * values
    return jnp.clip(values, min=-most, max=most).astype(kind)


def setup_inputs(seed: int = 0) -> dict:
    streams_of = jax.random.split(jax.random.key(seed), 16)
    return {
        "density": gaussian(streams_of[0], (LEAVES, PAN), 1.0, 6.0, ((0, 128),), jnp.float32),
        "positions": draw_positions(jax.random.fold_in(streams_of[15], 71), 0),
        "counts": draw_counts(jax.random.fold_in(streams_of[15], 71), 0),
        "leaf_parent": touch_ends(jax.random.randint(streams_of[3], (LEAVES,), 0, PAR), jax.random.fold_in(streams_of[3], 1), 0, PAR - 1).astype(jnp.int32),
        "child_pos": touch_ends(jax.random.randint(streams_of[4], (LEAVES,), 0, 8), jax.random.fold_in(streams_of[4], 1), 0, 7).astype(jnp.int32),
        "send_slots": draw_send_slots(jax.random.fold_in(streams_of[15], 71), 0),
        "far_source": draw_far_source(jax.random.fold_in(streams_of[15], 71), 0),
        "far_type": touch_ends(jax.random.randint(streams_of[7], (LEAVES, NL), 0, NT), jax.random.fold_in(streams_of[7], 1), 0, NT - 1).astype(jnp.int32),
        "near_offset": draw_near_offset(jax.random.fold_in(streams_of[15], 71), 0),
        "near_dir": touch_ends(jax.random.randint(streams_of[9], (LEAVES, NB), 0, 27), jax.random.fold_in(streams_of[9], 1), 0, 26).astype(jnp.int32),
        "coarse_source": touch_ends(jax.random.randint(streams_of[10], (TOP, NC), 0, TOP), jax.random.fold_in(streams_of[10], 1), 0, TOP - 1).astype(jnp.int32),
        "coarse_type": touch_ends(jax.random.randint(streams_of[11], (TOP, NC), 0, NT), jax.random.fold_in(streams_of[11], 1), 0, NT - 1).astype(jnp.int32),
        "m2l": gaussian(streams_of[12], (NT, K, K), K ** -0.5, 0.375),
        "m2m": gaussian(streams_of[13], (8, K, K), (K * CHILDREN) ** -0.5, 0.03125),
        "l2l": gaussian(streams_of[14], (8, K, K), K ** -0.5, 0.375),
    }


KAPPA = 0.25
DELTA = 0.05
RADIUS = 2.0
HIGHEST_PRECISION = lax.Precision.HIGHEST

def check_points(number):
    middle = jnp.arange(number, dtype=jnp.float32) + 0.5
    height = 1.0 - 2.0 * middle / number
    radial = jnp.sqrt(jnp.maximum(1.0 - height * height, 0.0))
    azimuth = math.pi * (1.0 + math.sqrt(5.0)) * middle
    return RADIUS * jnp.stack([radial * jnp.cos(azimuth), radial * jnp.sin(azimuth), height])

def damped_green(squared):
    spread = jnp.sqrt(squared + DELTA * DELTA)
    return jnp.exp(-KAPPA * spread) / spread

def leaf_kernels(panel_xyz, checks):
    between = panel_xyz[:, :, :, None] - checks[None, :, None, :]
    return damped_green(lax.optimization_barrier(jnp.sum(between * between, axis=1))).astype(jnp.bfloat16)

def direction_shift(directions):
    return 2.0 * jnp.stack([directions // 9 - 1, directions // 3 % 3 - 1, directions % 3 - 1], axis=-1).astype(jnp.float32)

def near_field(target_xyz, sources, shifts):
    between = target_xyz[:, None, :, :, None] - sources[:, :, 0:3, None, :] - shifts[:, :, :, None, None]
    kernel = damped_green(lax.optimization_barrier(jnp.sum(between * between, axis=2))).astype(jnp.bfloat16)
    weights = sources[:, :, 3, :].astype(jnp.bfloat16)
    return jnp.einsum('bnpq,bnq->bp', kernel.astype(jnp.float32), weights.astype(jnp.float32), precision=HIGHEST_PRECISION)

def grouped_sum(entries, kinds, number):
    selector = (kinds[:, :, None] == jnp.arange(number, dtype=jnp.int32)[None, None, :]).astype(jnp.bfloat16)
    summed = jnp.einsum('bnt,bnk->btk', selector.astype(jnp.float32), entries.astype(jnp.bfloat16).astype(jnp.float32), precision=HIGHEST_PRECISION)
    return summed.astype(jnp.bfloat16)

def translate(grouped, table):
    rows = grouped.shape[0]
    return jnp.dot(grouped.reshape(rows, -1), table.reshape(-1, table.shape[2]), preferred_element_type=jnp.float32)

def by_child(values, children):
    chosen = children[:, None] == jnp.arange(8, dtype=jnp.int32)[None, :]
    return jnp.where(chosen[:, :, None], values[:, None, :], jnp.zeros((), values.dtype))

def reference(density, positions, counts, leaf_parent, child_pos, send_slots, far_source, far_type, near_offset, near_dir, coarse_source, coarse_type, m2l, m2m, l2l):
    occupied = jnp.arange(PAN, dtype=jnp.int32)[None, :] < counts[:, None]
    masked = jnp.where(occupied, density, jnp.zeros((), density.dtype))
    masked_low = masked.astype(jnp.bfloat16)
    checks = check_points(K)
    blocks = math.gcd(LEAVES, 64)

    def moment_block(pieces):
        panel_xyz, weights = pieces
        kernel = leaf_kernels(panel_xyz, checks)
        return jnp.einsum('bpk,bp->bk', kernel.astype(jnp.float32), weights.astype(jnp.float32), precision=HIGHEST_PRECISION) / math.sqrt(PAN)
    moments = lax.map(moment_block, (positions.reshape(-1, blocks, 3, PAN), masked_low.reshape(-1, blocks, PAN)))
    moments = moments.reshape(LEAVES, K).astype(jnp.bfloat16)

    def upward(pieces):
        moment_rows, children, parents = pieces
        translated = translate(by_child(moment_rows, children), m2m).astype(jnp.bfloat16)
        selector = (parents[None, :] == jnp.arange(PAR, dtype=jnp.int32)[:, None]).astype(jnp.bfloat16)
        return jnp.dot(selector, translated, preferred_element_type=jnp.float32)
    partials = lax.map(upward, (moments.reshape(DEVICES, LEAF_DEV, K), child_pos.reshape(DEVICES, LEAF_DEV), leaf_parent.reshape(DEVICES, LEAF_DEV)))
    parent_moments = lax.optimization_barrier(jnp.sum(partials.reshape(N_OCT, N_LEAF, PAR, K), axis=1)).reshape(TOP, K).astype(jnp.bfloat16)
    parent_local = translate(grouped_sum(parent_moments[coarse_source], coarse_type, NT), m2l).astype(jnp.bfloat16)

    def far_device(pieces):
        device, sources, kinds, parents, children = pieces
        owner = sources // CAP
        leaf_ids = owner * LEAF_DEV + send_slots[owner, device, sources % CAP]
        local = translate(grouped_sum(moments[leaf_ids], kinds, NT), m2l)
        group_rows = parent_local[device // N_LEAF * PAR + parents]
        return (local + translate(by_child(group_rows, children), l2l)).astype(jnp.bfloat16)
    expansions = lax.map(far_device, (jnp.arange(DEVICES, dtype=jnp.int32), far_source.reshape(DEVICES, LEAF_DEV, NL), far_type.reshape(DEVICES, LEAF_DEV, NL), leaf_parent.reshape(DEVICES, LEAF_DEV), child_pos.reshape(DEVICES, LEAF_DEV)))
    expansions = expansions.reshape(LEAVES, K)
    stacked = jnp.concatenate([positions, masked[:, None, :]], axis=1)
    small = math.gcd(LEAVES, 16)
    near_weight = 1.0 / math.sqrt(NB * PAN)

    def potential_block(pieces):
        first, panel_xyz, local_rows, offsets, directions = pieces
        targets = first + jnp.arange(small, dtype=jnp.int32)[:, None] + offsets
        sources = stacked[targets]
        near = near_field(panel_xyz, sources, direction_shift(directions))
        kernel = leaf_kernels(panel_xyz, checks)
        far = jnp.einsum('bpk,bk->bp', kernel.astype(jnp.float32), local_rows.astype(jnp.float32), precision=HIGHEST_PRECISION) / math.sqrt(K)
        return near_weight * near + far
    starts = jnp.arange(LEAVES // small, dtype=jnp.int32) * small
    fields = lax.map(potential_block, (starts, positions.reshape(-1, small, 3, PAN), expansions.reshape(-1, small, K), near_offset.reshape(-1, small, NB), near_dir.reshape(-1, small, NB)))
    fields = fields.reshape(LEAVES, PAN)
    return jnp.where(occupied, 0.5 * density + fields, jnp.zeros((), density.dtype))
```

```python
import functools
import math

import jax
import jax.numpy as jnp
import ml_dtypes
import numpy as np
from jax import lax
from jax.experimental import pallas as pl
from jax.experimental.pallas import tpu as pltpu
from jax.sharding import PartitionSpec as P

HW = 32
KAPPA = 0.25
DELTA = 0.05
RADIUS = 2.0
RATE = -KAPPA * math.log2(math.e)
ROWS = 32
BF = jnp.bfloat16
F32 = jnp.float32
VMEM = pl.BlockSpec(memory_space=pltpu.VMEM)
SMEM = pl.BlockSpec(memory_space=pltpu.SMEM)


def np_split(values, number):
    pieces = []
    rest = values.astype(np.float32)
    for _ in range(number):
        piece = rest.astype(ml_dtypes.bfloat16)
        pieces.append(piece)
        rest = rest - piece.astype(np.float32)
    return pieces


def check_rows(number):
    middle = np.arange(number, dtype=np.float32) + np.float32(0.5)
    height = (1.0 - 2.0 * middle / np.float32(number)).astype(np.float32)
    radial = np.sqrt(np.maximum(1.0 - height * height, 0.0)).astype(np.float32)
    azimuth = np.float32(math.pi * (1.0 + math.sqrt(5.0))) * middle
    points = RADIUS * np.stack([radial * np.cos(azimuth), radial * np.sin(azimuth), height])
    high, low = np_split(points, 2)
    high, low = high.astype(np.float32), low.astype(np.float32)
    rounded = high + low
    squares = np_split(np.sum(rounded * rounded, axis=0), 3)
    rows = np.zeros((ROWS, number), np.float32)
    rows[0:3], rows[3:6], rows[6:9], rows[9:12] = -2 * high, -2 * low, -2 * high, -2 * low
    for k in range(3):
        rows[12 + k] = squares[k].astype(np.float32)
    rows[15:18] = 1.0
    return rows.astype(ml_dtypes.bfloat16)


def shift_rows():
    scale = np.zeros((27, ROWS, 128), np.float32)
    add = np.zeros((27, ROWS, 128), np.float32)
    scale[:, 0:18] = 1.0
    scale[:, 31] = 1.0
    for d in range(27):
        shift = 2.0 * np.array([d // 9 - 1, d // 3 % 3 - 1, d % 3 - 1], np.float32)
        for k in range(3):
            scale[d, 18 + k] = -shift[k]
            scale[d, 21 + k] = -shift[k]
            add[d, 24 + k] = -2 * shift[k]
            add[d, 27 + k] = -2 * shift[k]
        add[d, 30] = np.sum(shift * shift)
    return scale.astype(ml_dtypes.bfloat16), add.astype(ml_dtypes.bfloat16)


def split(value):
    high = value.astype(BF).astype(F32)
    return high, value - high


def panel_rows(coords, weights):
    highs, lows, square = [], [], None
    for value in coords:
        high, rest = split(value)
        low = rest.astype(BF).astype(F32)
        highs.append(high)
        lows.append(low)
        rounded = high + low
        square = rounded * rounded if square is None else square + rounded * rounded
    one = jnp.ones_like(square)
    zero = jnp.zeros_like(square)

    def thirds(value):
        first, rest = split(value)
        second, rest = split(rest)
        return [first, second, rest]

    minus_high = [-2.0 * value for value in highs]
    minus_low = [-2.0 * value for value in lows]
    target = highs + highs + lows + lows + [one] * 3 + thirds(square + DELTA * DELTA)
    target += [one] * 6 + highs + lows + [one, zero]
    source = minus_high + minus_low + minus_high + minus_low + thirds(square) + [one] * 3
    source += minus_high + minus_low + [zero] * 7 + [weights]
    return target, source


def place_rows(rows, scratch, write):
    for r, value in enumerate(rows):
        scratch[pl.ds(r, 8, stride=ROWS), :] = value
    for u in range(8):
        write(u, scratch[u * ROWS : (u + 1) * ROWS, :].astype(BF))


def green(squared):
    low = squared.astype(BF)
    inverse = lax.rsqrt(low)
    return jnp.exp2((low * inverse) * BF(RATE)) * inverse


def dot(a, b, over=((1,), (0,))):
    return lax.dot_general(a, b, (over, ((), ())), preferred_element_type=F32)


def moments_kernel(
    slots_ref, pos_ref, dens_ref, counts_ref, code_ref, checks_ref, m2m_ref,
    target_ref, source_ref, weight_ref, send_ref, part_ref, moments_low, moments_high, scratch, spare,
):
    step = pl.program_id(0)
    leaves = pos_ref.shape[1]
    total = moments_low.shape[0]
    checks = checks_ref[...]
    lane = lax.broadcasted_iota(jnp.int32, (8, 128), 1)

    def build(group, carry):
        at = pl.ds(pl.multiple_of(group * 8, 8), 8)
        masked = jnp.where(lane < counts_ref[at, :], dens_ref[at, :], 0.0)
        weight_ref[at, :] = masked
        target, source = panel_rows([pos_ref[d, at, :] for d in range(3)], masked)

        def put_target(u, value):
            target_ref[group * 8 + u] = value

        def put_source(u, value):
            source_ref[group * 8 + u] = value

        place_rows(target, scratch, put_target)
        place_rows(source, spare, put_source)
        return carry

    lax.fori_loop(0, leaves // 8, build, 0)
    unroll = 16

    def expand(group, carry):
        for u in range(unroll):
            leaf = group * unroll + u
            kernel = green(dot(target_ref[leaf], checks, ((0,), (0,))))
            out = dot(source_ref[leaf][16:32], kernel)[15:16]
            low = (out * (1.0 / math.sqrt(128))).astype(BF).astype(F32)
            at = pl.ds(step * leaves + leaf, 1)
            moments_low[at, :], moments_high[at, :] = low[:, :128], low[:, 128:]
        return carry

    lax.fori_loop(0, leaves // unroll, expand, 0)

    @pl.when(step == pl.num_programs(0) - 1)
    def _():
        for partner in range(8):

            def pick(s, carry):
                slot = jnp.maximum(slots_ref[partner, s], 0)
                spare[pl.ds(s, 1), :] = moments_low[pl.ds(slot, 1), :]
                scratch[pl.ds(s, 1), :] = moments_high[pl.ds(slot, 1), :]
                return carry

            lax.fori_loop(0, 32, pick, 0, unroll=8)
            send_ref[partner] = jnp.concatenate(
                [spare[0:32, :], scratch[0:32, :]], axis=1
            ).astype(BF)
        low = jnp.concatenate([moments_low[...], moments_high[...]], axis=1).astype(BF)
        parents = part_ref.shape[0]
        acc = jnp.zeros(part_ref.shape, F32)
        for c in range(8):
            row = lax.broadcasted_iota(jnp.int32, (parents, total), 0) + c * parents
            chosen = jnp.where(row == code_ref[...], 1.0, 0.0).astype(BF)
            high, rest = split(dot(chosen, low))
            acc += dot(high.astype(BF), m2m_ref[c]) + dot(rest.astype(BF), m2m_ref[c])
        part_ref[...] = acc.astype(BF)


def halo_kernel(raw_ref, source_ref, scratch):
    def build(group, carry):
        at = pl.ds(pl.multiple_of(group * 8, 8), 8)
        _, source = panel_rows([raw_ref[d, at, :] for d in range(3)], raw_ref[3, at, :])

        def put_source(u, value):
            source_ref[group * 8 + u] = value

        place_rows(source, scratch, put_source)
        return carry

    lax.fori_loop(0, raw_ref.shape[1] // 8, build, 0)


def near_kernel(
    index_ref, dir_ref, target_ref, before_ref, source_ref, after_ref, scale_ref, add_ref,
    out_ref, window, sems,
):
    step = pl.program_id(0)
    leaves = target_ref.shape[0]
    total = source_ref.shape[0]

    @pl.when(step == 0)
    def _():
        copies = [
            pltpu.make_async_copy(before_ref, window.at[0:HW], sems.at[0]),
            pltpu.make_async_copy(source_ref, window.at[HW : HW + total], sems.at[1]),
            pltpu.make_async_copy(after_ref, window.at[HW + total : 2 * HW + total], sems.at[2]),
        ]
        for copy in copies:
            copy.start()
        for copy in copies:
            copy.wait()

    unroll = 16

    def one(leaf):
        whole = step * leaves + leaf
        rows, weights = [], []
        for j in range(4):
            base = window[index_ref[j, whole]]
            way = dir_ref[j, whole]
            rows.append(base * scale_ref[way] + add_ref[way])
            weights.append(base[16:32])
        kernel = green(dot(target_ref[leaf], jnp.concatenate(rows, 1), ((0,), (0,))))
        return dot(jnp.concatenate(weights, 1), kernel, ((1,), (1,)))[15:16]

    def body(group, carry):
        for u in range(unroll):
            leaf = group * unroll + u
            out_ref[pl.ds(leaf, 1), :] = one(leaf) * (1.0 / math.sqrt(512))
        return carry

    lax.fori_loop(0, leaves // unroll, body, 0)


def translate_kernel(
    far_ref, coarse_from_ref, coarse_to_ref, recv_ref, parents_ref, m2l_ref, l2l_ref,
    out_ref, z_low, z_high, groups_low, groups_high, parents_low, parents_high, acc,
    rows_low, rows_high,
):
    step = pl.program_id(0)
    count = m2l_ref.shape[0]
    received = recv_ref.shape[0]
    cells = acc.shape[0]
    entries, leaves = far_ref.shape
    coarse, _ = coarse_from_ref.shape

    @pl.when(step == 0)
    def _():
        groups_low[...] = jnp.zeros(groups_low.shape, F32)
        groups_high[...] = jnp.zeros(groups_high.shape, F32)
        parents_low[...] = parents_ref[:, :128].astype(F32)
        parents_high[...] = parents_ref[:, 128:].astype(F32)
        acc[...] = jnp.zeros(acc.shape, F32)

        def gather(q, carry):
            for j in range(coarse):
                at = pl.ds(coarse_to_ref[j, q], 1)
                row = pl.ds(coarse_from_ref[j, q], 1)
                groups_low[at, :] = groups_low[at, :] + parents_low[row, :]
                groups_high[at, :] = groups_high[at, :] + parents_high[row, :]
            return carry

        lax.fori_loop(0, cells, gather, 0)

    for t in range(count):
        kind = step * count + t
        at = pl.ds(pl.multiple_of(kind * cells, cells), cells)
        group = jnp.concatenate([groups_low[at, :], groups_high[at, :]], axis=1).astype(BF)
        table = m2l_ref[t]
        out = dot(recv_ref[...], table)
        at = pl.ds(pl.multiple_of(kind * received, received), received)
        z_low[at, :] = out[:, :128]
        z_high[at, :] = out[:, 128:]
        acc[...] += dot(group, table)

    @pl.when(step == pl.num_programs(0) - 1)
    def _():
        local = acc[...].astype(BF)
        first = received * count * pl.num_programs(0)
        for c in range(8):
            out = dot(local, l2l_ref[c])
            at = pl.ds(first + c * cells, cells)
            z_low[at, :] = out[:, :128]
            z_high[at, :] = out[:, 128:]

        def block(group, carry):
            for u in range(8):
                lows, highs = [None] * 4, [None] * 4
                for j in range(entries):
                    at = pl.ds(far_ref[j, group * 8 + u], 1)
                    low, high = z_low[at, :], z_high[at, :]
                    k = j % 4
                    lows[k] = low if lows[k] is None else lows[k] + low
                    highs[k] = high if highs[k] is None else highs[k] + high
                at = pl.ds(group * 8 + u, 1)
                rows_low[at, :] = (lows[0] + lows[1]) + (lows[2] + lows[3])
                rows_high[at, :] = (highs[0] + highs[1]) + (highs[2] + highs[3])
            return carry

        lax.fori_loop(0, leaves // 8, block, 0)
        out_ref[:, :128] = rows_low[...].astype(BF)
        out_ref[:, 128:] = rows_high[...].astype(BF)


def far_kernel(target_ref, checks_ref, exp_ref, near_ref, dens_ref, counts_ref, out_ref):
    leaves = target_ref.shape[0]
    unroll = 16
    lane = lax.broadcasted_iota(jnp.int32, (unroll, 128), 1)
    checks = checks_ref[...]

    def body(group, carry):
        at = pl.ds(pl.multiple_of(group * unroll, unroll), unroll)
        local = exp_ref[at, :]
        outs = []
        for u in range(unroll):
            kernel = green(dot(checks, target_ref[group * unroll + u]))
            outs.append(dot(local, kernel)[u : u + 1])
        far = jnp.concatenate(outs, 0) * (1.0 / math.sqrt(256))
        value = 0.5 * dens_ref[at, :] + near_ref[at, :] + far
        out_ref[at, :] = jnp.where(lane < counts_ref[at, :], value, 0.0)
        return carry

    lax.fori_loop(0, leaves // unroll, body, 0)


def params(mib=56):
    return pltpu.CompilerParams(vmem_limit_bytes=mib * 2**20)


def local(
    density, positions, counts, leaf_parent, child_pos, send_slots, far_source, far_type,
    near_offset, near_dir, coarse_source, coarse_type, m2l, m2m, l2l,
):
    leaves, panels = density.shape
    width = m2l.shape[1]
    kinds = m2l.shape[0]
    cells = coarse_source.shape[0]
    oct_size, leaf_size = lax.axis_size("oct"), lax.axis_size("leaf")
    group, place = lax.axis_index("oct"), lax.axis_index("leaf")
    cap = send_slots.shape[2]
    planes = positions.transpose(1, 0, 2)
    counts_column = counts[:, None]
    spread_counts = jnp.broadcast_to(counts_column, (leaves, panels))
    checks = check_rows(width)
    scale, add = shift_rows()

    lanes = jnp.arange(panels, dtype=jnp.int32)[None, :]

    def edge(begin):
        rows = slice(begin, begin + HW)
        masked = jnp.where(lanes < counts_column[rows], density[rows], 0.0)
        return jnp.concatenate([planes[:, rows], masked[None]], axis=0)

    up = [(i, i + 1) for i in range(leaf_size - 1)]
    down = [(i + 1, i) for i in range(leaf_size - 1)]
    before = lax.ppermute(edge(leaves - HW), "leaf", up)
    after = lax.ppermute(edge(0), "leaf", down)

    moves = [("leaf", k - 2) for k in range(5)]
    moves += [("oct", 1), ("oct", -1), ("oct", oct_size // 2)]
    targets = []
    for axis, by in moves:
        if axis == "leaf":
            targets.append(group * leaf_size + jnp.clip(place - by, 0, leaf_size - 1))
        else:
            targets.append((group - by) % oct_size * leaf_size + place)
    slots = jnp.stack([send_slots[0, target] for target in targets])
    code = (child_pos * cells + leaf_parent)[None, :]

    steps = 8
    block = leaves // steps
    target, source, weights, send, partial = pl.pallas_call(
        moments_kernel,
        grid=(steps,),
        in_specs=[
            SMEM,
            pl.BlockSpec((3, block, panels), lambda i: (0, i, 0)),
            pl.BlockSpec((block, panels), lambda i: (i, 0)),
            pl.BlockSpec((block, panels), lambda i: (i, 0)),
            VMEM, VMEM, VMEM,
        ],
        out_specs=[
            pl.BlockSpec((block, ROWS, panels), lambda i: (i, 0, 0)),
            pl.BlockSpec((block, ROWS, panels), lambda i: (i, 0, 0)),
            pl.BlockSpec((block, panels), lambda i: (i, 0)),
            VMEM, VMEM,
        ],
        out_shape=[
            jax.ShapeDtypeStruct((leaves, ROWS, panels), BF),
            jax.ShapeDtypeStruct((leaves, ROWS, panels), BF),
            jax.ShapeDtypeStruct((leaves, panels), F32),
            jax.ShapeDtypeStruct((8, cap, width), BF),
            jax.ShapeDtypeStruct((cells, width), BF),
        ],
        scratch_shapes=[
            pltpu.VMEM((leaves, 128), F32),
            pltpu.VMEM((leaves, 128), F32),
            pltpu.VMEM((8 * ROWS, panels), F32),
            pltpu.VMEM((8 * ROWS, panels), F32),
        ],
        compiler_params=params(),
        name="moments",
    )(slots, planes, density, spread_counts, code, checks, m2m)

    halo = pl.pallas_call(
        halo_kernel,
        in_specs=[VMEM],
        out_specs=VMEM,
        out_shape=jax.ShapeDtypeStruct((2 * HW, ROWS, panels), BF),
        scratch_shapes=[pltpu.VMEM((8 * ROWS, panels), F32)],
        compiler_params=params(),
        name="halo",
    )(jnp.concatenate([before, after], axis=1))

    pieces = []
    for k, (axis, by) in enumerate(moves):
        if axis == "leaf" and by == 0:
            pieces.append(send[k])
        elif axis == "leaf":
            pairs = [(i, i - by) for i in range(leaf_size) if 0 <= i - by < leaf_size]
            pieces.append(lax.ppermute(send[k], "leaf", pairs))
        else:
            pairs = [(i, (i - by) % oct_size) for i in range(oct_size)]
            pieces.append(lax.ppermute(send[k], "oct", pairs))
    received = jnp.concatenate(pieces, axis=0)

    group_parts = lax.all_gather(partial, "leaf", axis=0)
    group_sum = jnp.sum(group_parts.astype(F32), axis=0).astype(BF)
    every_parent = lax.all_gather(group_sum, "oct", axis=0, tiled=True)

    index = (jnp.arange(leaves, dtype=jnp.int32)[:, None] + near_offset + HW).T
    near = pl.pallas_call(
        near_kernel,
        grid=(steps,),
        in_specs=[
            SMEM, SMEM,
            pl.BlockSpec((block, ROWS, panels), lambda i: (i, 0, 0)),
            pl.BlockSpec(memory_space=pl.ANY),
            pl.BlockSpec(memory_space=pl.ANY),
            pl.BlockSpec(memory_space=pl.ANY),
            VMEM, VMEM,
        ],
        out_specs=pl.BlockSpec((block, panels), lambda i: (i, 0)),
        out_shape=jax.ShapeDtypeStruct((leaves, panels), F32),
        scratch_shapes=[
            pltpu.VMEM((leaves + 2 * HW, ROWS, panels), BF),
            pltpu.SemaphoreType.DMA((3,)),
        ],
        compiler_params=params(),
        name="near",
    )(index, near_dir.T, target, halo[:HW], source, halo[HW:], scale, add)

    owner, slot = far_source // cap, far_source % cap
    owner_group, owner_place = owner // leaf_size, owner % leaf_size
    partner = jnp.where(
        owner_group == group,
        owner_place - place + 2,
        jnp.where(
            owner_group == (group + 1) % oct_size,
            5,
            jnp.where(owner_group == (group + oct_size - 1) % oct_size, 6, 7),
        ),
    )
    far_rows = (far_type * 8 + partner) * cap + slot
    own_row = kinds * 8 * cap + child_pos * cells + leaf_parent
    far_rows = jnp.concatenate([far_rows.T, own_row[None, :]], axis=0)
    coarse_to = (coarse_type * cells + jnp.arange(cells, dtype=jnp.int32)[:, None]).T
    span = 8
    expansions = pl.pallas_call(
        translate_kernel,
        grid=(kinds // span,),
        in_specs=[
            SMEM, SMEM, SMEM, VMEM, VMEM,
            pl.BlockSpec((span, width, width), lambda i: (i, 0, 0)),
            VMEM,
        ],
        out_specs=VMEM,
        out_shape=jax.ShapeDtypeStruct((leaves, width), BF),
        scratch_shapes=[
            pltpu.VMEM((kinds * 8 * cap + 8 * cells, 128), F32),
            pltpu.VMEM((kinds * 8 * cap + 8 * cells, 128), F32),
            pltpu.VMEM((kinds * cells, 128), F32),
            pltpu.VMEM((kinds * cells, 128), F32),
            pltpu.VMEM((oct_size * cells, 128), F32),
            pltpu.VMEM((oct_size * cells, 128), F32),
            pltpu.VMEM((cells, width), F32),
            pltpu.VMEM((leaves, 128), F32),
            pltpu.VMEM((leaves, 128), F32),
        ],
        compiler_params=params(),
        name="translate",
    )(far_rows, coarse_source.T, coarse_to, received, every_parent, m2l, l2l)

    return pl.pallas_call(
        far_kernel,
        grid=(steps,),
        in_specs=[
            pl.BlockSpec((block, ROWS, panels), lambda i: (i, 0, 0)),
            VMEM,
            pl.BlockSpec((block, width), lambda i: (i, 0)),
            pl.BlockSpec((block, panels), lambda i: (i, 0)),
            pl.BlockSpec((block, panels), lambda i: (i, 0)),
            pl.BlockSpec((block, panels), lambda i: (i, 0)),
        ],
        out_specs=pl.BlockSpec((block, panels), lambda i: (i, 0)),
        out_shape=jax.ShapeDtypeStruct((leaves, panels), F32),
        compiler_params=params(),
        name="far",
    )(target, checks.T, expansions, near, density, spread_counts)


def solution(mesh):
    both = ("oct", "leaf")
    placed = (
        P(both, None), P(both, None, None), P(both), P(both), P(both), P(both, None, None),
        P(both, None), P(both, None), P(both, None), P(both, None),
        P("oct", None), P("oct", None), P(), P(), P(),
    )
    return jax.shard_map(
        local, mesh=mesh, in_specs=placed, out_specs=P(both, None), check_vma=False
    )
```

```python
import functools
import math

import jax
import jax.numpy as jnp
import ml_dtypes
import numpy as np
from jax import lax
from jax.experimental import pallas as pl
from jax.experimental.pallas import tpu as pltpu
from jax.sharding import PartitionSpec as P

HW = 32
KAPPA = 0.25
DELTA = 0.05
RADIUS = 2.0
RATE = -KAPPA * math.log2(math.e)
ROWS = 32
BF = jnp.bfloat16
F32 = jnp.float32
VMEM = pl.BlockSpec(memory_space=pltpu.VMEM)
SMEM = pl.BlockSpec(memory_space=pltpu.SMEM)


def np_split(values, number):
    pieces = []
    rest = values.astype(np.float32)
    for _ in range(number):
        piece = rest.astype(ml_dtypes.bfloat16)
        pieces.append(piece)
        rest = rest - piece.astype(np.float32)
    return pieces


def check_rows(number):
    middle = np.arange(number, dtype=np.float32) + np.float32(0.5)
    height = (1.0 - 2.0 * middle / np.float32(number)).astype(np.float32)
    radial = np.sqrt(np.maximum(1.0 - height * height, 0.0)).astype(np.float32)
    azimuth = np.float32(math.pi * (1.0 + math.sqrt(5.0))) * middle
    points = RADIUS * np.stack([radial * np.cos(azimuth), radial * np.sin(azimuth), height])
    high, low = np_split(points, 2)
    high, low = high.astype(np.float32), low.astype(np.float32)
    rounded = high + low
    squares = np_split(np.sum(rounded * rounded, axis=0), 3)
    rows = np.zeros((ROWS, number), np.float32)
    rows[0:3], rows[3:6], rows[6:9], rows[9:12] = -2 * high, -2 * low, -2 * high, -2 * low
    for k in range(3):
        rows[12 + k] = squares[k].astype(np.float32)
    rows[15:18] = 1.0
    return rows.astype(ml_dtypes.bfloat16)


def shift_rows():
    scale = np.zeros((27, ROWS, 128), np.float32)
    add = np.zeros((27, ROWS, 128), np.float32)
    scale[:, 0:18] = 1.0
    scale[:, 31] = 1.0
    for d in range(27):
        shift = 2.0 * np.array([d // 9 - 1, d // 3 % 3 - 1, d % 3 - 1], np.float32)
        for k in range(3):
            scale[d, 18 + k] = -shift[k]
            scale[d, 21 + k] = -shift[k]
            add[d, 24 + k] = -2 * shift[k]
            add[d, 27 + k] = -2 * shift[k]
        add[d, 30] = np.sum(shift * shift)
    return scale.astype(ml_dtypes.bfloat16), add.astype(ml_dtypes.bfloat16)


def split(value):
    high = value.astype(BF).astype(F32)
    return high, value - high


def panel_rows(coords, weights):
    highs, lows, square = [], [], None
    for value in coords:
        high, rest = split(value)
        low = rest.astype(BF).astype(F32)
        highs.append(high)
        lows.append(low)
        rounded = high + low
        square = rounded * rounded if square is None else square + rounded * rounded
    one = jnp.ones_like(square)
    zero = jnp.zeros_like(square)

    def thirds(value):
        first, rest = split(value)
        second, rest = split(rest)
        return [first, second, rest]

    minus_high = [-2.0 * value for value in highs]
    minus_low = [-2.0 * value for value in lows]
    target = highs + highs + lows + lows + [one] * 3 + thirds(square + DELTA * DELTA)
    target += [one] * 6 + highs + lows + [one, zero]
    source = minus_high + minus_low + minus_high + minus_low + thirds(square) + [one] * 3
    source += minus_high + minus_low + [zero] * 7 + [weights]
    return target, source


def place_rows(rows, scratch, write):
    for r, value in enumerate(rows):
        scratch[pl.ds(r, 8, stride=ROWS), :] = value
    for u in range(8):
        write(u, scratch[u * ROWS : (u + 1) * ROWS, :].astype(BF))


def green(squared):
    low = squared.astype(BF)
    inverse = lax.rsqrt(low)
    return jnp.exp2((low * inverse) * BF(RATE)) * inverse


def dot(a, b, over=((1,), (0,))):
    return lax.dot_general(a, b, (over, ((), ())), preferred_element_type=F32)


def moments_kernel(
    slots_ref, pos_ref, dens_ref, counts_ref, code_ref, checks_ref, m2m_ref,
    target_ref, source_ref, tile_ref, part_ref, *rest,
):
    send_refs, (weights, moments_low, moments_high, scratch, spare) = rest[:8], rest[8:]
    step = pl.program_id(0)
    leaves = pos_ref.shape[1]
    total = moments_low.shape[0]
    checks = checks_ref[...]
    lane = lax.broadcasted_iota(jnp.int32, (8, 128), 1)

    def build(group, carry):
        at = pl.ds(pl.multiple_of(group * 8, 8), 8)
        masked = jnp.where(lane < counts_ref[at, :], dens_ref[at, :], 0.0)
        weights[at, :] = masked
        target, source = panel_rows([pos_ref[d, at, :] for d in range(3)], masked)

        def put_target(u, value):
            target_ref[group * 8 + u] = value

        def put_source(u, value):
            source_ref[group * 8 + u] = value

        place_rows(target, scratch, put_target)
        place_rows(source, spare, put_source)
        return carry

    lax.fori_loop(0, leaves // 8, build, 0)
    row = lax.broadcasted_iota(jnp.int32, (16, 128), 0)

    def squares(leaf):
        return dot(checks, jnp.concatenate([target_ref[leaf + u] for u in range(4)], axis=1))

    def finish(first, part, kernel, sums):
        tile_ref[:, pl.ds(pl.multiple_of((first + part * 4) * 128, 512), 512)] = kernel
        block = part // 4
        value = weights[pl.ds(pl.multiple_of(first + block * 16, 16), 16), :]
        spread = [jnp.where(row == part % 4 * 4 + u, value, 0.0) for u in range(4)]
        out = dot(jnp.concatenate(spread, axis=1).astype(BF), kernel, ((1,), (1,)))
        sums[block] = out if part % 4 == 0 else sums[block] + out
        if part % 4 == 3:
            low = (sums[block] * (1.0 / math.sqrt(128))).astype(BF).astype(F32)
            at = pl.ds(pl.multiple_of(step * leaves + first + block * 16, 16), 16)
            moments_low[at, :], moments_high[at, :] = low[:, :128], low[:, 128:]

    def expand(group, carry):
        first = group * span
        ahead, kernels, sums = {}, {}, {}
        for s in range(span // 4 + 2):
            if s < span // 4:
                ahead[s] = squares(first + s * 4)
            if 0 <= s - 1 < span // 4:
                kernels[s - 1] = green(ahead.pop(s - 1))
            if 0 <= s - 2:
                finish(first, s - 2, kernels.pop(s - 2), sums)
        return carry

    span = 64
    lax.fori_loop(0, leaves // span, expand, 0)

    @pl.when(step == pl.num_programs(0) - 1)
    def _():
        for partner in range(8):

            def pick(s, carry):
                slot = jnp.maximum(slots_ref[partner, s], 0)
                spare[pl.ds(s, 1), :] = moments_low[pl.ds(slot, 1), :]
                scratch[pl.ds(s, 1), :] = moments_high[pl.ds(slot, 1), :]
                return carry

            lax.fori_loop(0, 32, pick, 0, unroll=8)
            send_refs[partner][...] = jnp.concatenate(
                [spare[0:32, :], scratch[0:32, :]], axis=1
            ).astype(BF)
        low = jnp.concatenate([moments_low[...], moments_high[...]], axis=1).astype(BF)
        parents = part_ref.shape[0]
        acc = jnp.zeros(part_ref.shape, F32)
        for c in range(8):
            row = lax.broadcasted_iota(jnp.int32, (parents, total), 0) + c * parents
            chosen = jnp.where(row == code_ref[...], 1.0, 0.0).astype(BF)
            high, rest = split(dot(chosen, low))
            acc += dot(high.astype(BF), m2m_ref[c]) + dot(rest.astype(BF), m2m_ref[c])
        part_ref[...] = acc.astype(BF)


def halo_kernel(raw_ref, source_ref, scratch):
    def build(group, carry):
        at = pl.ds(pl.multiple_of(group * 8, 8), 8)
        _, source = panel_rows([raw_ref[d, at, :] for d in range(3)], raw_ref[3, at, :])

        def put_source(u, value):
            source_ref[group * 8 + u] = value

        place_rows(source, scratch, put_source)
        return carry

    lax.fori_loop(0, raw_ref.shape[1] // 8, build, 0)


def near_kernel(begin, index_ref, dir_ref, target_ref, *refs):
    *parts, scale_ref, add_ref, out_ref, window, sems = refs
    leaves = target_ref.shape[0]
    copies, at = [], 0
    for k, part in enumerate(parts):
        size = part.shape[0]
        if size == HW:
            source = part
        else:
            low = max(begin - HW, 0)
            size = min(begin + leaves + HW, size) - low
            source = part.at[low : low + size]
        copies.append(pltpu.make_async_copy(source, window.at[at : at + size], sems.at[k]))
        at += size
    for copy in copies:
        copy.start()
    for copy in copies:
        copy.wait()

    def squares(leaf):
        whole = begin + leaf
        rows, weights = [], []
        for j in range(4):
            base = window[index_ref[j, whole]]
            way = dir_ref[j, whole]
            rows.append(base * scale_ref[way] + add_ref[way])
            weights.append(base[16:32])
        value = dot(target_ref[leaf], jnp.concatenate(rows, 1), ((0,), (0,)))
        return value, jnp.concatenate(weights, 1)

    unroll, depth = 32, 2

    def body(group, carry):
        first = group * unroll
        ahead = []
        for u in range(unroll + depth):
            if u < unroll:
                ahead.append(squares(first + u))
            if u >= depth:
                value, weights = ahead[u - depth]
                out = dot(weights, green(value), ((1,), (1,)))[15:16]
                out_ref[pl.ds(first + u - depth, 1), :] = out * (1.0 / math.sqrt(512))
        return carry

    lax.fori_loop(0, leaves // unroll, body, 0)


def translate_kernel(
    far_ref, coarse_from_ref, coarse_to_ref, recv_ref, parents_ref, m2l_ref, l2l_ref,
    out_ref, z_low, z_high, groups_low, groups_high, parents_low, parents_high, acc,
    rows_low, rows_high,
):
    step = pl.program_id(0)
    count = m2l_ref.shape[0]
    received = recv_ref.shape[0]
    cells = acc.shape[0]
    entries, leaves = far_ref.shape
    coarse, _ = coarse_from_ref.shape

    @pl.when(step == 0)
    def _():
        groups_low[...] = jnp.zeros(groups_low.shape, F32)
        groups_high[...] = jnp.zeros(groups_high.shape, F32)
        parents_low[...] = parents_ref[:, :128].astype(F32)
        parents_high[...] = parents_ref[:, 128:].astype(F32)
        acc[...] = jnp.zeros(acc.shape, F32)

        def gather(q, carry):
            for j in range(coarse):
                at = pl.ds(coarse_to_ref[j, q], 1)
                row = pl.ds(coarse_from_ref[j, q], 1)
                groups_low[at, :] = groups_low[at, :] + parents_low[row, :]
                groups_high[at, :] = groups_high[at, :] + parents_high[row, :]
            return carry

        lax.fori_loop(0, cells, gather, 0)

    for t in range(count):
        kind = step * count + t
        at = pl.ds(pl.multiple_of(kind * cells, cells), cells)
        group = jnp.concatenate([groups_low[at, :], groups_high[at, :]], axis=1).astype(BF)
        table = m2l_ref[t]
        out = dot(recv_ref[...], table)
        at = pl.ds(pl.multiple_of(kind * received, received), received)
        z_low[at, :] = out[:, :128]
        z_high[at, :] = out[:, 128:]
        acc[...] += dot(group, table)

    @pl.when(step == pl.num_programs(0) - 1)
    def _():
        local = acc[...].astype(BF)
        first = received * count * pl.num_programs(0)
        for c in range(8):
            out = dot(local, l2l_ref[c])
            at = pl.ds(first + c * cells, cells)
            z_low[at, :] = out[:, :128]
            z_high[at, :] = out[:, 128:]

        def block(group, carry):
            for u in range(8):
                lows, highs = [None] * 4, [None] * 4
                for j in range(entries):
                    at = pl.ds(far_ref[j, group * 8 + u], 1)
                    low, high = z_low[at, :], z_high[at, :]
                    k = j % 4
                    lows[k] = low if lows[k] is None else lows[k] + low
                    highs[k] = high if highs[k] is None else highs[k] + high
                at = pl.ds(group * 8 + u, 1)
                rows_low[at, :] = (lows[0] + lows[1]) + (lows[2] + lows[3])
                rows_high[at, :] = (highs[0] + highs[1]) + (highs[2] + highs[3])
            return carry

        lax.fori_loop(0, leaves // 8, block, 0)
        out_ref[:, :128] = rows_low[...].astype(BF)
        out_ref[:, 128:] = rows_high[...].astype(BF)


def far_kernel(tile_ref, exp_ref, dens_ref, counts_ref, *refs):
    near_refs, out_ref = refs[:-1], refs[-1]
    step = pl.program_id(0)
    leaves = out_ref.shape[0]
    unroll = 16
    lane = lax.broadcasted_iota(jnp.int32, (unroll, 128), 1)
    row = lax.broadcasted_iota(jnp.int32, (unroll, 128), 0)
    per = pl.num_programs(0) // len(near_refs)
    for group in range(leaves // unroll):
        at = pl.ds(group * unroll, unroll)
        out = dot(exp_ref[at, :], tile_ref[:, group * unroll * 128 : (group + 1) * unroll * 128])
        far = jnp.zeros((unroll, 128), F32)
        for u in range(unroll):
            far = jnp.where(row == u, out[:, u * 128 : (u + 1) * 128], far)
        near = near_refs[0][pl.ds(pl.multiple_of(step % per * leaves + group * unroll, 16), 16), :]
        for k in range(1, len(near_refs)):
            other = near_refs[k][pl.ds(pl.multiple_of(step % per * leaves + group * unroll, 16), 16), :]
            near = jnp.where(step // per == k, other, near)
        value = 0.5 * dens_ref[at, :] + near + far * (1.0 / math.sqrt(256))
        out_ref[at, :] = jnp.where(lane < counts_ref[at, :], value, 0.0)


def params(mib=56):
    return pltpu.CompilerParams(vmem_limit_bytes=mib * 2**20)


def local(
    density, positions, counts, leaf_parent, child_pos, send_slots, far_source, far_type,
    near_offset, near_dir, coarse_source, coarse_type, m2l, m2m, l2l,
):
    leaves, panels = density.shape
    width = m2l.shape[1]
    kinds = m2l.shape[0]
    cells = coarse_source.shape[0]
    oct_size, leaf_size = lax.axis_size("oct"), lax.axis_size("leaf")
    group, place = lax.axis_index("oct"), lax.axis_index("leaf")
    cap = send_slots.shape[2]
    planes = positions.transpose(1, 0, 2)
    counts_column = counts[:, None]
    spread_counts = jnp.broadcast_to(counts_column, (leaves, panels))
    checks = check_rows(width)
    scale, add = shift_rows()

    lanes = jnp.arange(panels, dtype=jnp.int32)[None, :]

    def edge(begin):
        rows = slice(begin, begin + HW)
        masked = jnp.where(lanes < counts_column[rows], density[rows], 0.0)
        return jnp.concatenate([planes[:, rows], masked[None]], axis=0)

    up = [(i, i + 1) for i in range(leaf_size - 1)]
    down = [(i + 1, i) for i in range(leaf_size - 1)]
    before = lax.ppermute(edge(leaves - HW), "leaf", up)
    after = lax.ppermute(edge(0), "leaf", down)

    moves = [("leaf", k - 2) for k in range(5)]
    moves += [("oct", 1), ("oct", -1), ("oct", oct_size // 2)]
    targets = []
    for axis, by in moves:
        if axis == "leaf":
            targets.append(group * leaf_size + jnp.clip(place - by, 0, leaf_size - 1))
        else:
            targets.append((group - by) % oct_size * leaf_size + place)
    slots = jnp.stack([send_slots[0, target] for target in targets])
    code = (child_pos * cells + leaf_parent)[None, :]

    steps = 8
    block = leaves // steps
    chunk = leaves // 4
    target, source, tile, partial, *send = pl.pallas_call(
        moments_kernel,
        grid=(steps,),
        in_specs=[
            SMEM,
            pl.BlockSpec((3, block, panels), lambda i: (0, i, 0)),
            pl.BlockSpec((block, panels), lambda i: (i, 0)),
            pl.BlockSpec((block, panels), lambda i: (i, 0)),
            VMEM, VMEM, VMEM,
        ],
        out_specs=[
            pl.BlockSpec((block, ROWS, panels), lambda i: (i, 0, 0)),
            pl.BlockSpec((block, ROWS, panels), lambda i: (i, 0, 0)),
            pl.BlockSpec((width, block * panels), lambda i: (0, i)),
        ]
        + [VMEM] * 9,
        out_shape=[
            jax.ShapeDtypeStruct((leaves, ROWS, panels), BF),
            jax.ShapeDtypeStruct((leaves, ROWS, panels), BF),
            jax.ShapeDtypeStruct((width, leaves * panels), BF),
            jax.ShapeDtypeStruct((cells, width), BF),
        ]
        + [jax.ShapeDtypeStruct((cap, width), BF)] * 8,
        scratch_shapes=[
            pltpu.VMEM((block, 128), F32),
            pltpu.VMEM((leaves, 128), F32),
            pltpu.VMEM((leaves, 128), F32),
            pltpu.VMEM((8 * ROWS, panels), F32),
            pltpu.VMEM((8 * ROWS, panels), F32),
        ],
        compiler_params=params(),
        name="moments",
    )(slots, planes, density, spread_counts, code, checks.T, m2m)

    halo = pl.pallas_call(
        halo_kernel,
        in_specs=[VMEM],
        out_specs=VMEM,
        out_shape=jax.ShapeDtypeStruct((2 * HW, ROWS, panels), BF),
        scratch_shapes=[pltpu.VMEM((8 * ROWS, panels), F32)],
        compiler_params=params(),
        name="halo",
    )(jnp.concatenate([before, after], axis=1))

    pieces = []
    for k, (axis, by) in enumerate(moves):
        if axis == "leaf" and by == 0:
            pieces.append(send[k])
        elif axis == "leaf":
            pairs = [(i, i - by) for i in range(leaf_size) if 0 <= i - by < leaf_size]
            pieces.append(lax.ppermute(send[k], "leaf", pairs))
        else:
            pairs = [(i, (i - by) % oct_size) for i in range(oct_size)]
            pieces.append(lax.ppermute(send[k], "oct", pairs))
    received = jnp.concatenate(pieces, axis=0)

    index = (jnp.arange(leaves, dtype=jnp.int32)[:, None] % chunk + near_offset + HW).T
    ways = near_dir.T

    def near_part(begin):
        if begin == 0:
            parts = [halo[:HW], source]
        elif begin + chunk == leaves:
            parts = [source, halo[HW:]]
        else:
            parts = [source]
        return pl.pallas_call(
            functools.partial(near_kernel, begin),
            grid=(1,),
            in_specs=[
                SMEM, SMEM,
                pl.BlockSpec((chunk, ROWS, panels), lambda i: (begin // chunk, 0, 0)),
            ]
            + [pl.BlockSpec(memory_space=pl.ANY)] * len(parts)
            + [VMEM, VMEM],
            out_specs=VMEM,
            out_shape=jax.ShapeDtypeStruct((chunk, panels), F32),
            scratch_shapes=[
                pltpu.VMEM((chunk + 2 * HW, ROWS, panels), BF),
                pltpu.SemaphoreType.DMA((2,)),
            ],
            compiler_params=params(),
            cost_estimate=pl.CostEstimate(
                flops=10**10, bytes_accessed=10**6, transcendentals=chunk * 2 * 65536
            ),
            name="near",
        )(index, ways, target, *parts, scale, add)

    inner = 4

    def exchange(value, number, other):
        got = [value.astype(F32)]
        for by in range(1, number):
            pairs = [(i, other(i, by)) for i in range(leaf_size)]
            got.append(lax.ppermute(value, "leaf", pairs).astype(F32))
        return got

    near = []
    fours = exchange(partial, inner, lambda i, by: i // inner * inner + (i + by) % inner)
    near.append(near_part(0))
    near[0], *fours = lax.optimization_barrier((near[0], *fours))
    total = sum(fours[1:], fours[0]).astype(BF)
    over = leaf_size // inner
    sixteen = exchange(total, over, lambda i, by: (i + by * inner) % leaf_size)
    sixteen[0], source, target = lax.optimization_barrier((sixteen[0], source, target))
    near.append(near_part(chunk))
    near[1], *sixteen = lax.optimization_barrier((near[1], *sixteen))
    total = sum(sixteen[1:], sixteen[0]).astype(BF)
    others = []
    for by in range(1, oct_size):
        pairs = [(i, (i + by) % oct_size) for i in range(oct_size)]
        others.append(lax.ppermute(total, "oct", pairs))
    total, source, target = lax.optimization_barrier((total, source, target))
    for k in range(2, leaves // chunk):
        near.append(near_part(k * chunk))
    *near, received, total = lax.optimization_barrier((*near, received, total))
    others = lax.optimization_barrier((near[-1], *others))[1:]
    every_parent = jnp.concatenate([total, *others], axis=0)

    owner, slot = far_source // cap, far_source % cap
    owner_group, owner_place = owner // leaf_size, owner % leaf_size
    partner = jnp.where(
        owner_group == group,
        owner_place - place + 2,
        jnp.where(
            owner_group == (group + 1) % oct_size,
            5,
            jnp.where(owner_group == (group + oct_size - 1) % oct_size, 6, 7),
        ),
    )
    far_rows = (far_type * 8 + partner) * cap + slot
    own_row = kinds * 8 * cap + child_pos * cells + leaf_parent
    far_rows = jnp.concatenate([far_rows.T, own_row[None, :]], axis=0)
    coarse_from = (group - coarse_source // cells) % oct_size * cells + coarse_source % cells
    coarse_to = (coarse_type * cells + jnp.arange(cells, dtype=jnp.int32)[:, None]).T
    span = 8
    expansions = pl.pallas_call(
        translate_kernel,
        grid=(kinds // span,),
        in_specs=[
            SMEM, SMEM, SMEM, VMEM, VMEM,
            pl.BlockSpec((span, width, width), lambda i: (i, 0, 0)),
            VMEM,
        ],
        out_specs=VMEM,
        out_shape=jax.ShapeDtypeStruct((leaves, width), BF),
        scratch_shapes=[
            pltpu.VMEM((kinds * 8 * cap + 8 * cells, 128), F32),
            pltpu.VMEM((kinds * 8 * cap + 8 * cells, 128), F32),
            pltpu.VMEM((kinds * cells, 128), F32),
            pltpu.VMEM((kinds * cells, 128), F32),
            pltpu.VMEM((oct_size * cells, 128), F32),
            pltpu.VMEM((oct_size * cells, 128), F32),
            pltpu.VMEM((cells, width), F32),
            pltpu.VMEM((leaves, 128), F32),
            pltpu.VMEM((leaves, 128), F32),
        ],
        compiler_params=params(),
        name="translate",
    )(far_rows, coarse_from.T, coarse_to, received, every_parent, m2l, l2l)

    return pl.pallas_call(
        far_kernel,
        grid=(steps,),
        in_specs=[
            pl.BlockSpec((width, block * panels), lambda i: (0, i)),
            pl.BlockSpec((block, width), lambda i: (i, 0)),
            pl.BlockSpec((block, panels), lambda i: (i, 0)),
            pl.BlockSpec((block, panels), lambda i: (i, 0)),
        ]
        + [VMEM] * len(near),
        out_specs=pl.BlockSpec((block, panels), lambda i: (i, 0)),
        out_shape=jax.ShapeDtypeStruct((leaves, panels), F32),
        compiler_params=params(),
        name="far",
    )(tile, expansions, density, spread_counts, *near)


def solution(mesh):
    both = ("oct", "leaf")
    placed = (
        P(both, None), P(both, None, None), P(both), P(both), P(both), P(both, None, None),
        P(both, None), P(both, None), P(both, None), P(both, None),
        P("oct", None), P("oct", None), P(), P(), P(),
    )
    return jax.shard_map(
        local, mesh=mesh, in_specs=placed, out_specs=P(both, None), check_vma=False
    )
```

```python
import functools
import math

import jax
import jax.numpy as jnp
import ml_dtypes
import numpy as np
from jax import lax
from jax.experimental import pallas as pl
from jax.experimental.pallas import tpu as pltpu
from jax.sharding import PartitionSpec as P

HW = 32
KAPPA = 0.25
DELTA = 0.05
RADIUS = 2.0
RATE = -KAPPA * math.log2(math.e)
ROWS = 32
BF = jnp.bfloat16
F32 = jnp.float32
VMEM = pl.BlockSpec(memory_space=pltpu.VMEM)
SMEM = pl.BlockSpec(memory_space=pltpu.SMEM)


def np_split(values, number):
    pieces = []
    rest = values.astype(np.float32)
    for _ in range(number):
        piece = rest.astype(ml_dtypes.bfloat16)
        pieces.append(piece)
        rest = rest - piece.astype(np.float32)
    return pieces


def check_rows(number):
    middle = np.arange(number, dtype=np.float32) + np.float32(0.5)
    height = (1.0 - 2.0 * middle / np.float32(number)).astype(np.float32)
    radial = np.sqrt(np.maximum(1.0 - height * height, 0.0)).astype(np.float32)
    azimuth = np.float32(math.pi * (1.0 + math.sqrt(5.0))) * middle
    points = RADIUS * np.stack([radial * np.cos(azimuth), radial * np.sin(azimuth), height])
    high, low = np_split(points, 2)
    high, low = high.astype(np.float32), low.astype(np.float32)
    rounded = high + low
    squares = np_split(np.sum(rounded * rounded, axis=0), 3)
    rows = np.zeros((ROWS, number), np.float32)
    rows[0:3], rows[3:6], rows[6:9], rows[9:12] = -2 * high, -2 * low, -2 * high, -2 * low
    for k in range(3):
        rows[12 + k] = squares[k].astype(np.float32)
    rows[15:18] = 1.0
    return rows.astype(ml_dtypes.bfloat16)


def shift_rows():
    scale = np.zeros((27, ROWS, 128), np.float32)
    add = np.zeros((27, ROWS, 128), np.float32)
    scale[:, 0:18] = 1.0
    scale[:, 31] = 1.0
    for d in range(27):
        shift = 2.0 * np.array([d // 9 - 1, d // 3 % 3 - 1, d % 3 - 1], np.float32)
        for k in range(3):
            scale[d, 18 + k] = -shift[k]
            scale[d, 21 + k] = -shift[k]
            add[d, 24 + k] = -2 * shift[k]
            add[d, 27 + k] = -2 * shift[k]
        add[d, 30] = np.sum(shift * shift)
    return scale.astype(ml_dtypes.bfloat16), add.astype(ml_dtypes.bfloat16)


def split(value):
    high = value.astype(BF).astype(F32)
    return high, value - high


def panel_rows(coords, weights):
    highs, lows, square = [], [], None
    for value in coords:
        high, rest = split(value)
        low = rest.astype(BF).astype(F32)
        highs.append(high)
        lows.append(low)
        rounded = high + low
        square = rounded * rounded if square is None else square + rounded * rounded
    one = jnp.ones_like(square)
    zero = jnp.zeros_like(square)

    def thirds(value):
        first, rest = split(value)
        second, rest = split(rest)
        return [first, second, rest]

    minus_high = [-2.0 * value for value in highs]
    minus_low = [-2.0 * value for value in lows]
    target = highs + highs + lows + lows + [one] * 3 + thirds(square + DELTA * DELTA)
    target += [one] * 6 + highs + lows + [one, zero]
    source = minus_high + minus_low + minus_high + minus_low + thirds(square) + [one] * 3
    source += minus_high + minus_low + [zero] * 7 + [weights]
    return target, source


def spread(ref, first, number):
    row = lax.broadcasted_iota(jnp.int32, (number, 128), 0)
    value = jnp.full((number, 128), ref[first], jnp.int32)
    for u in range(1, number):
        value = jnp.where(row == u, ref[first + u], value)
    return value


def place_rows(rows, scratch, write):
    for r, value in enumerate(rows):
        scratch[pl.ds(r, 8, stride=ROWS), :] = value
    for u in range(8):
        write(u, scratch[u * ROWS : (u + 1) * ROWS, :].astype(BF))


def green(squared):
    low = squared.astype(BF)
    inverse = lax.rsqrt(low)
    return jnp.exp2((low * inverse) * BF(RATE)) * inverse


def dot(a, b, over=((1,), (0,))):
    return lax.dot_general(a, b, (over, ((), ())), preferred_element_type=F32)


def moments_kernel(
    sizes, slots_ref, counts_ref, pos_ref, dens_ref, code_ref, checks_ref, m2m_ref,
    target_ref, source_ref, tile_ref, first_ref, last_ref, *rest,
):
    send_refs, part_refs = rest[:8], (rest[8], rest[0], rest[1])
    weights, moments_low, moments_high, scratch, spare = rest[9:]
    step = pl.program_id(0)
    leaves = pos_ref.shape[1]
    total = moments_low.shape[0]
    checks = checks_ref[...]
    lane = lax.broadcasted_iota(jnp.int32, (8, 128), 1)

    def build(group, carry):
        at = pl.ds(pl.multiple_of(group * 8, 8), 8)
        masked = jnp.where(lane < spread(counts_ref, step * leaves + group * 8, 8), dens_ref[at, :], 0.0)
        weights[at, :] = masked
        target, source = panel_rows([pos_ref[d, at, :] for d in range(3)], masked)

        def put_target(u, value):
            target_ref[group * 8 + u] = value

        def put_source(u, value):
            source_ref[group * 8 + u] = value

        place_rows(target, scratch, put_target)
        place_rows(source, spare, put_source)
        return carry

    lax.fori_loop(0, leaves // 8, build, 0)
    row = lax.broadcasted_iota(jnp.int32, (16, 128), 0)

    def squares(leaf):
        return dot(checks, jnp.concatenate([target_ref[leaf + u] for u in range(4)], axis=1))

    def finish(first, part, kernel, sums):
        tile_ref[:, pl.ds(pl.multiple_of((first + part * 4) * 128, 512), 512)] = kernel
        block = part // 4
        value = weights[pl.ds(pl.multiple_of(first + block * 16, 16), 16), :]
        apart = [jnp.where(row == part % 4 * 4 + u, value, 0.0) for u in range(4)]
        out = dot(jnp.concatenate(apart, axis=1).astype(BF), kernel, ((1,), (1,)))
        sums[block] = out if part % 4 == 0 else sums[block] + out
        if part % 4 == 3:
            low = (sums[block] * (1.0 / math.sqrt(128))).astype(BF).astype(F32)
            at = pl.ds(pl.multiple_of(step * leaves + first + block * 16, 16), 16)
            moments_low[at, :], moments_high[at, :] = low[:, :128], low[:, 128:]

    def expand(group, carry):
        first = group * span
        ahead, kernels, sums = {}, {}, {}
        for s in range(span // 4 + 2):
            if s < span // 4:
                ahead[s] = squares(first + s * 4)
            if 0 <= s - 1 < span // 4:
                kernels[s - 1] = green(ahead.pop(s - 1))
            if 0 <= s - 2:
                finish(first, s - 2, kernels.pop(s - 2), sums)
        return carry

    span = 64
    lax.fori_loop(0, leaves // span, expand, 0)

    @pl.when(step == 0)
    def _():
        first_ref[...] = source_ref[0:HW]

    @pl.when(step == pl.num_programs(0) - 1)
    def _():
        last_ref[...] = source_ref[leaves - HW :]
        group, place = lax.axis_index("oct"), lax.axis_index("leaf")
        oct_size, leaf_size = sizes
        for partner in range(8):
            if partner < 5:
                other = jnp.clip(place + 2 - partner, 0, leaf_size - 1)
                other = group * leaf_size + other
            else:
                by = (oct_size - 1, 1, oct_size // 2)[partner - 5]
                other = lax.rem(group + by, oct_size) * leaf_size + place

            def pick(s, carry):
                slot = jnp.maximum(slots_ref[s, other], 0)
                spare[pl.ds(s, 1), :] = moments_low[pl.ds(slot, 1), :]
                scratch[pl.ds(s, 1), :] = moments_high[pl.ds(slot, 1), :]
                return carry

            lax.fori_loop(0, 32, pick, 0, unroll=8)
            send_refs[partner][-32:, :] = jnp.concatenate(
                [spare[0:32, :], scratch[0:32, :]], axis=1
            ).astype(BF)
        low = jnp.concatenate([moments_low[...], moments_high[...]], axis=1).astype(BF)
        parents = part_refs[0].shape[0]
        acc = jnp.zeros(part_refs[0].shape, F32)
        for c in range(8):
            row = lax.broadcasted_iota(jnp.int32, (parents, total), 0) + c * parents
            chosen = jnp.where(row == code_ref[...], 1.0, 0.0).astype(BF)
            high, rest = split(dot(chosen, low))
            acc += dot(high.astype(BF), m2m_ref[c]) + dot(rest.astype(BF), m2m_ref[c])
        for part_ref in part_refs:
            part_ref[0:parents, :] = acc.astype(BF)


def near_kernel(begin, offset_ref, dir_ref, target_ref, *refs):
    *parts, scale_ref, add_ref, out_ref, window, sems = refs
    leaves = target_ref.shape[0]
    copies, at = [], 0
    for k, part in enumerate(parts):
        size = part.shape[0]
        if size == HW:
            source = part
        else:
            low = max(begin - HW, 0)
            size = min(begin + leaves + HW, size) - low
            source = part.at[low : low + size]
        copies.append(pltpu.make_async_copy(source, window.at[at : at + size], sems.at[k]))
        at += size
    for copy in copies:
        copy.start()
    for copy in copies:
        copy.wait()

    def squares(leaf):
        whole = begin + leaf
        rows, weights = [], []
        for j in range(4):
            base = window[leaf + HW + offset_ref[j, whole]]
            way = dir_ref[j, whole]
            rows.append(base * scale_ref[way] + add_ref[way])
            weights.append(base[16:32])
        value = dot(target_ref[leaf], jnp.concatenate(rows, 1), ((0,), (0,)))
        return value, jnp.concatenate(weights, 1)

    unroll, depth = 32, 2

    def body(group, carry):
        first = group * unroll
        ahead = []
        for u in range(unroll + depth):
            if u < unroll:
                ahead.append(squares(first + u))
            if u >= depth:
                value, weights = ahead[u - depth]
                out = dot(weights, green(value), ((1,), (1,)))[15:16]
                out_ref[pl.ds(first + u - depth, 1), :] = out * (1.0 / math.sqrt(512))
        return carry

    lax.fori_loop(0, leaves // unroll, body, 0)


def translate_kernel(
    far_ref, coarse_from_ref, coarse_to_ref, *refs,
):
    recv_refs, parent_refs, (m2l_ref, l2l_ref, out_ref) = refs[:8], refs[8:12], refs[12:15]
    z_low, z_high, groups_low, groups_high, parents_low, parents_high = refs[15:21]
    acc, rows_low, rows_high, recv_ref = refs[21:]
    step = pl.program_id(0)
    count = m2l_ref.shape[0]
    received = recv_ref.shape[0]
    cells = acc.shape[0]
    leaves = rows_low.shape[0]
    entries = far_ref.shape[0] // leaves
    coarse, _ = coarse_from_ref.shape

    @pl.when(step == 0)
    def _():
        groups_low[...] = jnp.zeros(groups_low.shape, F32)
        groups_high[...] = jnp.zeros(groups_high.shape, F32)
        oct_size = parents_low.shape[0] // cells
        before = 0
        for part in parent_refs:
            for k in range(part.shape[0] // cells):
                owner = lax.rem(lax.axis_index("oct") + oct_size - before, oct_size)
                at = pl.ds(pl.multiple_of(owner * cells, cells), cells)
                piece = part[k * cells : (k + 1) * cells, :].astype(F32)
                parents_low[at, :], parents_high[at, :] = piece[:, :128], piece[:, 128:]
                before += 1
        for k, part in enumerate(recv_refs):
            recv_ref[k * 32 : (k + 1) * 32, :] = part[-32:, :]
        acc[...] = jnp.zeros(acc.shape, F32)

        def gather(q, carry):
            for j in range(coarse):
                at = pl.ds(coarse_to_ref[j, q] * cells + q, 1)
                row = pl.ds(coarse_from_ref[j, q], 1)
                groups_low[at, :] = groups_low[at, :] + parents_low[row, :]
                groups_high[at, :] = groups_high[at, :] + parents_high[row, :]
            return carry

        lax.fori_loop(0, cells, gather, 0)

    for t in range(count):
        kind = step * count + t
        at = pl.ds(pl.multiple_of(kind * cells, cells), cells)
        group = jnp.concatenate([groups_low[at, :], groups_high[at, :]], axis=1).astype(BF)
        table = m2l_ref[t]
        out = dot(recv_ref[...], table)
        at = pl.ds(pl.multiple_of(kind * received, received), received)
        z_low[at, :] = out[:, :128]
        z_high[at, :] = out[:, 128:]
        acc[...] += dot(group, table)

    @pl.when(step == pl.num_programs(0) - 1)
    def _():
        local = acc[...].astype(BF)
        first = received * count * pl.num_programs(0)
        for c in range(8):
            out = dot(local, l2l_ref[c])
            at = pl.ds(first + c * cells, cells)
            z_low[at, :] = out[:, :128]
            z_high[at, :] = out[:, 128:]

        def block(group, carry):
            for u in range(8):
                lows, highs = [None] * 4, [None] * 4
                for j in range(entries):
                    at = pl.ds(far_ref[j * leaves + group * 8 + u], 1)
                    low, high = z_low[at, :], z_high[at, :]
                    k = j % 4
                    lows[k] = low if lows[k] is None else lows[k] + low
                    highs[k] = high if highs[k] is None else highs[k] + high
                at = pl.ds(group * 8 + u, 1)
                rows_low[at, :] = (lows[0] + lows[1]) + (lows[2] + lows[3])
                rows_high[at, :] = (highs[0] + highs[1]) + (highs[2] + highs[3])
            return carry

        lax.fori_loop(0, leaves // 8, block, 0)
        out_ref[:, :128] = rows_low[...].astype(BF)
        out_ref[:, 128:] = rows_high[...].astype(BF)


def far_kernel(counts_ref, tile_ref, exp_ref, dens_ref, *refs):
    near_refs, out_ref = refs[:-1], refs[-1]
    step = pl.program_id(0)
    leaves = out_ref.shape[0]
    unroll = 16
    lane = lax.broadcasted_iota(jnp.int32, (unroll, 128), 1)
    row = lax.broadcasted_iota(jnp.int32, (unroll, 128), 0)
    per = pl.num_programs(0) // len(near_refs)
    for group in range(leaves // unroll):
        at = pl.ds(group * unroll, unroll)
        out = dot(exp_ref[at, :], tile_ref[:, group * unroll * 128 : (group + 1) * unroll * 128])
        far = jnp.zeros((unroll, 128), F32)
        for u in range(unroll):
            far = jnp.where(row == u, out[:, u * 128 : (u + 1) * 128], far)
        near = near_refs[0][pl.ds(pl.multiple_of(step % per * leaves + group * unroll, 16), 16), :]
        for k in range(1, len(near_refs)):
            other = near_refs[k][pl.ds(pl.multiple_of(step % per * leaves + group * unroll, 16), 16), :]
            near = jnp.where(step // per == k, other, near)
        value = 0.5 * dens_ref[at, :] + near + far * (1.0 / math.sqrt(256))
        counts = spread(counts_ref, step * leaves + group * unroll, unroll)
        out_ref[at, :] = jnp.where(lane < counts, value, 0.0)


def params(mib=56):
    return pltpu.CompilerParams(vmem_limit_bytes=mib * 2**20)


def local(
    density, positions, counts, leaf_parent, child_pos, send_slots, far_source, far_type,
    near_offset, near_dir, coarse_source, coarse_type, m2l, m2m, l2l,
):
    leaves, panels = density.shape
    width = m2l.shape[1]
    kinds = m2l.shape[0]
    cells = coarse_source.shape[0]
    oct_size, leaf_size = lax.axis_size("oct"), lax.axis_size("leaf")
    group, place = lax.axis_index("oct"), lax.axis_index("leaf")
    cap = send_slots.shape[2]
    planes = positions.transpose(1, 0, 2)
    checks = check_rows(width)
    scale, add = shift_rows()

    code = (child_pos * cells + leaf_parent)[None, :]

    steps = 8
    block = leaves // steps
    chunk = leaves // 4
    target, source, tile, first, last, *send = pl.pallas_call(
        functools.partial(moments_kernel, (oct_size, leaf_size)),
        grid=(steps,),
        in_specs=[
            SMEM, SMEM,
            pl.BlockSpec((3, block, panels), lambda i: (0, i, 0)),
            pl.BlockSpec((block, panels), lambda i: (i, 0)),
            VMEM, VMEM, VMEM,
        ],
        out_specs=[
            pl.BlockSpec((block, ROWS, panels), lambda i: (i, 0, 0)),
            pl.BlockSpec((block, ROWS, panels), lambda i: (i, 0, 0)),
            pl.BlockSpec((width, block * panels), lambda i: (0, i)),
        ]
        + [VMEM] * 11,
        out_shape=[
            jax.ShapeDtypeStruct((leaves, ROWS, panels), BF),
            jax.ShapeDtypeStruct((leaves, ROWS, panels), BF),
            jax.ShapeDtypeStruct((width, leaves * panels), BF),
        ]
        + [jax.ShapeDtypeStruct((HW, ROWS, panels), BF)] * 2
        + [jax.ShapeDtypeStruct((cells + cap, width), BF)] * 2
        + [jax.ShapeDtypeStruct((cap, width), BF)] * 6
        + [jax.ShapeDtypeStruct((cells, width), BF)],
        scratch_shapes=[
            pltpu.VMEM((block, 128), F32),
            pltpu.VMEM((leaves, 128), F32),
            pltpu.VMEM((leaves, 128), F32),
            pltpu.VMEM((8 * ROWS, panels), F32),
            pltpu.VMEM((8 * ROWS, panels), F32),
        ],
        compiler_params=params(),
        name="moments",
    )(send_slots[0].T, counts, planes, density, code, checks.T, m2m)

    offsets = near_offset.T
    ways = near_dir.T

    def near_part(begin):
        if begin == 0:
            parts = [before, source]
        elif begin + chunk == leaves:
            parts = [source, after]
        else:
            parts = [source]
        return pl.pallas_call(
            functools.partial(near_kernel, begin),
            grid=(1,),
            in_specs=[
                SMEM, SMEM,
                pl.BlockSpec((chunk, ROWS, panels), lambda i: (begin // chunk, 0, 0)),
            ]
            + [pl.BlockSpec(memory_space=pl.ANY)] * len(parts)
            + [VMEM, VMEM],
            out_specs=VMEM,
            out_shape=jax.ShapeDtypeStruct((chunk, panels), F32),
            scratch_shapes=[
                pltpu.VMEM((chunk + 2 * HW, ROWS, panels), BF),
                pltpu.SemaphoreType.DMA((2,)),
            ],
            compiler_params=params(),
            cost_estimate=pl.CostEstimate(
                flops=10**10, bytes_accessed=10**6, transcendentals=chunk * 2 * 65536
            ),
            name="near",
        )(offsets, ways, target, *parts, scale, add)

    def shifted(value, axis, by):
        size = lax.axis_size(axis)
        return lax.ppermute(value, axis, [(i, (i + by) % size) for i in range(size)])

    def moved(value, by):
        pairs = [(i, i + by) for i in range(leaf_size) if 0 <= i + by < leaf_size]
        return lax.ppermute(value, "leaf", pairs)

    def added(pieces):
        total = pieces[0].astype(F32)
        for piece in pieces[1:]:
            total = total + piece.astype(F32)
        return total.astype(BF)

    partial = send[8]
    by_two = shifted(send[0], "leaf", 2)
    by_one = shifted(send[1], "leaf", 1)
    by_three = shifted(partial, "leaf", 3)
    back_one, back_two = moved(send[3], -1), moved(send[4], -2)
    before, after = moved(last, 1), moved(first, -1)
    near = [None] * 4
    near[1] = near_part(chunk)
    near[1], by_one, by_two, by_three, back_one, back_two, before, after = lax.optimization_barrier(
        (near[1], by_one, by_two, by_three, back_one, back_two, before, after)
    )
    four = added([partial, by_one[:cells], by_two[:cells], by_three])
    strides = [shifted(four, "leaf", by) for by in (4, 8, 12)]
    across = [
        shifted(send[5], "oct", -1), shifted(send[6], "oct", 1),
        shifted(send[7], "oct", oct_size // 2),
    ]
    four, source, target = lax.optimization_barrier((four, source, target))
    near[2] = near_part(2 * chunk)
    near[2], four, *moving = lax.optimization_barrier((near[2], four, *strides, *across))
    strides, across = moving[:3], moving[3:]
    total = added([four, *strides])
    lower = shifted(total, "oct", 1)
    total, source, target = lax.optimization_barrier((total, source, target))
    near[0] = near_part(0)
    near[0], total, lower = lax.optimization_barrier((near[0], total, lower))
    pair = jnp.concatenate([total, lower], axis=0)
    pairs = [shifted(pair, "oct", by) for by in (2, 4, 6)]
    pair, source, target = lax.optimization_barrier((pair, source, target))
    near[3] = near_part(3 * chunk)
    near[3], pair, *pairs = lax.optimization_barrier((near[3], pair, *pairs))
    every_parent = [pair, *pairs]
    received = [by_two, by_one, send[2], back_one, back_two, *across]

    owner, slot = far_source // cap, far_source % cap
    owner_group, owner_place = owner // leaf_size, owner % leaf_size
    partner = jnp.where(
        owner_group == group,
        owner_place - place + 2,
        jnp.where(
            owner_group == (group + 1) % oct_size,
            5,
            jnp.where(owner_group == (group + oct_size - 1) % oct_size, 6, 7),
        ),
    )
    far_rows = (far_type * 8 + partner) * cap + slot
    own_row = kinds * 8 * cap + child_pos * cells + leaf_parent
    far_rows = jnp.concatenate([far_rows.T.reshape(-1), own_row])
    span = 8
    expansions = pl.pallas_call(
        translate_kernel,
        grid=(kinds // span,),
        in_specs=[
            SMEM, SMEM, SMEM,
        ]
        + [VMEM] * 12
        + [
            pl.BlockSpec((span, width, width), lambda i: (i, 0, 0)),
            VMEM,
        ],
        out_specs=VMEM,
        out_shape=jax.ShapeDtypeStruct((leaves, width), BF),
        scratch_shapes=[
            pltpu.VMEM((kinds * 8 * cap + 8 * cells, 128), F32),
            pltpu.VMEM((kinds * 8 * cap + 8 * cells, 128), F32),
            pltpu.VMEM((kinds * cells, 128), F32),
            pltpu.VMEM((kinds * cells, 128), F32),
            pltpu.VMEM((oct_size * cells, 128), F32),
            pltpu.VMEM((oct_size * cells, 128), F32),
            pltpu.VMEM((cells, width), F32),
            pltpu.VMEM((leaves, 128), F32),
            pltpu.VMEM((leaves, 128), F32),
            pltpu.VMEM((8 * cap, width), BF),
        ],
        compiler_params=params(),
        name="translate",
    )(far_rows, coarse_source.T, coarse_type.T, *received, *every_parent, m2l, l2l)

    return pl.pallas_call(
        far_kernel,
        grid=(steps,),
        in_specs=[
            SMEM,
            pl.BlockSpec((width, block * panels), lambda i: (0, i)),
            pl.BlockSpec((block, width), lambda i: (i, 0)),
            pl.BlockSpec((block, panels), lambda i: (i, 0)),
        ]
        + [VMEM] * len(near),
        out_specs=pl.BlockSpec((block, panels), lambda i: (i, 0)),
        out_shape=jax.ShapeDtypeStruct((leaves, panels), F32),
        compiler_params=params(),
        name="far",
    )(counts, tile, expansions, density, *near)


def solution(mesh):
    both = ("oct", "leaf")
    placed = (
        P(both, None), P(both, None, None), P(both), P(both), P(both), P(both, None, None),
        P(both, None), P(both, None), P(both, None), P(both, None),
        P("oct", None), P("oct", None), P(), P(), P(),
    )
    return jax.shard_map(
        local, mesh=mesh, in_specs=placed, out_specs=P(both, None), check_vma=False
    )
```

```python
import functools
import math

import jax
import jax.numpy as jnp
import ml_dtypes
import numpy as np
from jax import lax
from jax.experimental import pallas as pl
from jax.experimental.pallas import tpu as pltpu
from jax.sharding import PartitionSpec as P

HW = 32
KAPPA = 0.25
DELTA = 0.05
RADIUS = 2.0
RATE = -KAPPA * math.log2(math.e)
ROWS = 32
PITCH = 36
BF = jnp.bfloat16
F32 = jnp.float32
VMEM = pl.BlockSpec(memory_space=pltpu.VMEM)
SMEM = pl.BlockSpec(memory_space=pltpu.SMEM)


def np_split(values, number):
    pieces = []
    rest = values.astype(np.float32)
    for _ in range(number):
        piece = rest.astype(ml_dtypes.bfloat16)
        pieces.append(piece)
        rest = rest - piece.astype(np.float32)
    return pieces


def check_rows(number):
    middle = np.arange(number, dtype=np.float32) + np.float32(0.5)
    height = (1.0 - 2.0 * middle / np.float32(number)).astype(np.float32)
    radial = np.sqrt(np.maximum(1.0 - height * height, 0.0)).astype(np.float32)
    azimuth = np.float32(math.pi * (1.0 + math.sqrt(5.0))) * middle
    points = RADIUS * np.stack([radial * np.cos(azimuth), radial * np.sin(azimuth), height])
    high, low = np_split(points, 2)
    high, low = high.astype(np.float32), low.astype(np.float32)
    rounded = high + low
    squares = np_split(np.sum(rounded * rounded, axis=0), 3)
    rows = np.zeros((ROWS, number), np.float32)
    rows[0:3], rows[3:6], rows[6:9], rows[9:12] = -2 * high, -2 * low, -2 * high, -2 * low
    for k in range(3):
        rows[12 + k] = squares[k].astype(np.float32)
    rows[15:18] = 1.0
    return rows.astype(ml_dtypes.bfloat16)


def shift_rows():
    scale = np.zeros((27, ROWS, 128), np.float32)
    add = np.zeros((27, ROWS, 128), np.float32)
    scale[:, 0:18] = 1.0
    scale[:, 31] = 1.0
    for d in range(27):
        shift = 2.0 * np.array([d // 9 - 1, d // 3 % 3 - 1, d % 3 - 1], np.float32)
        for k in range(3):
            scale[d, 18 + k] = -shift[k]
            scale[d, 21 + k] = -shift[k]
            add[d, 24 + k] = -2 * shift[k]
            add[d, 27 + k] = -2 * shift[k]
        add[d, 30] = np.sum(shift * shift)
    return scale.astype(ml_dtypes.bfloat16), add.astype(ml_dtypes.bfloat16)


def split(value):
    high = value.astype(BF).astype(F32)
    return high, value - high


def panel_rows(coords, weights):
    highs, lows, square = [], [], None
    for value in coords:
        high, rest = split(value)
        low = rest.astype(BF).astype(F32)
        highs.append(high)
        lows.append(low)
        rounded = high + low
        square = rounded * rounded if square is None else square + rounded * rounded
    one = jnp.ones_like(square)
    zero = jnp.zeros_like(square)

    def thirds(value):
        first, rest = split(value)
        second, rest = split(rest)
        return [first, second, rest]

    minus_high = [-2.0 * value for value in highs]
    minus_low = [-2.0 * value for value in lows]
    target = highs + highs + lows + lows + [one] * 3 + thirds(square + DELTA * DELTA)
    target += [one] * 6 + highs + lows + [one, zero]
    source = minus_high + minus_low + minus_high + minus_low + thirds(square) + [one] * 3
    source += minus_high + minus_low + [zero] * 7 + [weights]
    return target, source


def spread(ref, first, number):
    row = lax.broadcasted_iota(jnp.int32, (number, 128), 0)
    value = jnp.full((number, 128), ref[first], jnp.int32)
    for u in range(1, number):
        value = jnp.where(row == u, ref[first + u], value)
    return value


def place_rows(rows, scratch, write):
    for r, value in enumerate(rows):
        scratch[pl.ds(r, 8, stride=PITCH), :] = value
    for u in range(8):
        write(u, scratch[u * PITCH : u * PITCH + ROWS, :].astype(BF))


def green(squared):
    low = squared.astype(BF)
    inverse = lax.rsqrt(low)
    return jnp.exp2((low * inverse) * BF(RATE)) * inverse


def dot(a, b, over=((1,), (0,))):
    return lax.dot_general(a, b, (over, ((), ())), preferred_element_type=F32)


def moments_kernel(
    sizes, slots_ref, counts_ref, pos_ref, dens_ref, code_ref, checks_ref, m2m_ref,
    target_ref, source_ref, tile_ref, first_ref, last_ref, *rest,
):
    send_refs, part_refs = rest[:8], (rest[8], rest[0], rest[1])
    weights, moments_low, moments_high, scratch, spare = rest[9:]
    step = pl.program_id(0)
    leaves = pos_ref.shape[1]
    total = moments_low.shape[0]
    checks = checks_ref[...]
    lane = lax.broadcasted_iota(jnp.int32, (8, 128), 1)

    def build(group, carry):
        at = pl.ds(pl.multiple_of(group * 8, 8), 8)
        masked = jnp.where(lane < spread(counts_ref, step * leaves + group * 8, 8), dens_ref[at, :], 0.0)
        weights[at, :] = masked
        target, source = panel_rows([pos_ref[d, at, :] for d in range(3)], masked)

        def put_target(u, value):
            target_ref[group * 8 + u] = value

        def put_source(u, value):
            source_ref[group * 8 + u] = value

        place_rows(target, scratch, put_target)
        place_rows(source, spare, put_source)
        return carry

    lax.fori_loop(0, leaves // 8, build, 0)
    row = lax.broadcasted_iota(jnp.int32, (16, 128), 0)

    def squares(leaf):
        return dot(checks, jnp.concatenate([target_ref[leaf + u] for u in range(4)], axis=1))

    def finish(first, part, kernel, sums):
        tile_ref[:, pl.ds(pl.multiple_of((first + part * 4) * 128, 512), 512)] = kernel
        block = part // 4
        value = weights[pl.ds(pl.multiple_of(first + block * 16, 16), 16), :]
        apart = [jnp.where(row == part % 4 * 4 + u, value, 0.0) for u in range(4)]
        out = dot(jnp.concatenate(apart, axis=1).astype(BF), kernel, ((1,), (1,)))
        sums[block] = out if part % 4 == 0 else sums[block] + out
        if part % 4 == 3:
            low = (sums[block] * (1.0 / math.sqrt(128))).astype(BF).astype(F32)
            at = pl.ds(pl.multiple_of(step * leaves + first + block * 16, 16), 16)
            moments_low[at, :], moments_high[at, :] = low[:, :128], low[:, 128:]

    def expand(group, carry):
        first = group * span
        ahead, kernels, sums = {}, {}, {}
        for s in range(span // 4 + 2):
            if s < span // 4:
                ahead[s] = squares(first + s * 4)
            if 0 <= s - 1 < span // 4:
                kernels[s - 1] = green(ahead.pop(s - 1))
            if 0 <= s - 2:
                finish(first, s - 2, kernels.pop(s - 2), sums)
        return carry

    span = 64
    lax.fori_loop(0, leaves // span, expand, 0)

    @pl.when(step == 0)
    def _():
        first_ref[...] = source_ref[0:HW]

    @pl.when(step == pl.num_programs(0) - 1)
    def _():
        last_ref[...] = source_ref[leaves - HW :]
        group, place = lax.axis_index("oct"), lax.axis_index("leaf")
        oct_size, leaf_size = sizes
        for partner in range(8):
            if partner < 5:
                other = jnp.clip(place + 2 - partner, 0, leaf_size - 1)
                other = group * leaf_size + other
            else:
                by = (oct_size - 1, 1, oct_size // 2)[partner - 5]
                other = lax.rem(group + by, oct_size) * leaf_size + place

            def pick(s, carry):
                slot = jnp.maximum(slots_ref[s, other], 0)
                spare[pl.ds(s, 1), :] = moments_low[pl.ds(slot, 1), :]
                scratch[pl.ds(s, 1), :] = moments_high[pl.ds(slot, 1), :]
                return carry

            lax.fori_loop(0, 32, pick, 0, unroll=8)
            send_refs[partner][-32:, :] = jnp.concatenate(
                [spare[0:32, :], scratch[0:32, :]], axis=1
            ).astype(BF)
        low = jnp.concatenate([moments_low[...], moments_high[...]], axis=1).astype(BF)
        parents = part_refs[0].shape[0]
        acc = jnp.zeros(part_refs[0].shape, F32)
        for c in range(8):
            row = lax.broadcasted_iota(jnp.int32, (parents, total), 0) + c * parents
            chosen = jnp.where(row == code_ref[...], 1.0, 0.0).astype(BF)
            high, rest = split(dot(chosen, low))
            acc += dot(high.astype(BF), m2m_ref[c]) + dot(rest.astype(BF), m2m_ref[c])
        for part_ref in part_refs:
            part_ref[0:parents, :] = acc.astype(BF)


def load_window(begin, target_ref, parts, target, window, sems):
    leaves = target.shape[0]
    copies = [pltpu.make_async_copy(target_ref.at[begin : begin + leaves], target, sems.at[2])]
    at = 0
    for k, part in enumerate(parts):
        size = part.shape[0]
        if size != HW:
            low = max(begin - HW, 0)
            size = min(begin + leaves + HW, size) - low
            part = part.at[low : low + size]
        copies.append(pltpu.make_async_copy(part, window.at[at : at + size], sems.at[k]))
        at += size
    for copy in copies:
        copy.start()
    return copies


def near_leaves(begin, first, number, refs, beside=None):
    offset_ref, dir_ref, scale_ref, add_ref, target, window, out_ref = refs

    def squares(leaf):
        whole = begin + leaf
        rows, weights = [], []
        for j in range(4):
            base = window[leaf + HW + offset_ref[j, whole]]
            way = dir_ref[j, whole]
            rows.append(base * scale_ref[way] + add_ref[way])
            weights.append(base[16:32])
        value = dot(target[leaf], jnp.concatenate(rows, 1), ((0,), (0,)))
        return value, jnp.concatenate(weights, 1)

    depth = 2
    ahead = []
    for u in range(number + depth):
        if u < number:
            ahead.append(squares(first + u))
            if beside is not None:
                beside(u)
        if u >= depth:
            value, weights = ahead[u - depth]
            ahead[u - depth] = None
            out = dot(weights, green(value), ((1,), (1,)))[15:16]
            out_ref[pl.ds(first + u - depth, 1), :] = out * (1.0 / math.sqrt(512))


def near_kernel(begin, offset_ref, dir_ref, scale_ref, add_ref, target_ref, *refs):
    *parts, out_ref, target, window, sems = refs
    for copy in load_window(begin, target_ref, parts, target, window, sems):
        copy.wait()

    def body(group, carry):
        own = (offset_ref, dir_ref, scale_ref, add_ref, target, window, out_ref)
        near_leaves(begin, group * 32, 32, own)
        return carry

    lax.fori_loop(0, target.shape[0] // 32, body, 0)


def translate_kernel(
    begin, offset_ref, dir_ref, far_ref, coarse_from_ref, coarse_to_ref,
    scale_ref, add_ref, l2l_ref, target_ref, source_ref, after_ref, m2l_ref, *refs,
):
    recv_refs, parent_refs, (near_ref, out_ref) = refs[:8], refs[8:12], refs[12:14]
    z_low, z_high, groups_low, groups_high, parents_low, parents_high = refs[14:20]
    acc, rows_low, rows_high, recv_ref, target, window, table, sems, table_sems = refs[20:]
    pieces = table_sems.shape[0]
    kinds = table.shape[0]
    span = kinds // pieces
    received = recv_ref.shape[0]
    cells = acc.shape[0]
    leaves = rows_low.shape[0]
    entries = far_ref.shape[0] // leaves
    coarse, _ = coarse_from_ref.shape

    loads = [
        pltpu.make_async_copy(
            m2l_ref.at[k * span : (k + 1) * span], table.at[k * span : (k + 1) * span],
            table_sems.at[k],
        )
        for k in range(pieces)
    ]
    for load in loads:
        load.start()
    copies = load_window(begin, target_ref, [source_ref, after_ref], target, window, sems)
    groups_low[...] = jnp.zeros(groups_low.shape, F32)
    groups_high[...] = jnp.zeros(groups_high.shape, F32)
    acc[...] = jnp.zeros(acc.shape, F32)
    oct_size = parents_low.shape[0] // cells
    before = 0
    for part in parent_refs:
        for k in range(part.shape[0] // cells):
            owner = lax.rem(lax.axis_index("oct") + oct_size - before, oct_size)
            at = pl.ds(pl.multiple_of(owner * cells, cells), cells)
            piece = part[k * cells : (k + 1) * cells, :].astype(F32)
            parents_low[at, :], parents_high[at, :] = piece[:, :128], piece[:, 128:]
            before += 1
    for k, part in enumerate(recv_refs):
        recv_ref[k * 32 : (k + 1) * 32, :] = part[-32:, :]

    def gather(q, carry):
        for j in range(coarse):
            at = pl.ds(coarse_to_ref[j, q] * cells + q, 1)
            row = pl.ds(coarse_from_ref[j, q], 1)
            groups_low[at, :] = groups_low[at, :] + parents_low[row, :]
            groups_high[at, :] = groups_high[at, :] + parents_high[row, :]
        return carry

    lax.fori_loop(0, cells, gather, 0)
    for k in range(pieces):
        loads[k].wait()

        def spread_out(t, carry):
            kind = k * span + t
            at = pl.ds(pl.multiple_of(kind * cells, cells), cells)
            group = jnp.concatenate([groups_low[at, :], groups_high[at, :]], axis=1).astype(BF)
            out = dot(recv_ref[...], table[kind])
            at = pl.ds(pl.multiple_of(kind * received, received), received)
            z_low[at, :] = out[:, :128]
            z_high[at, :] = out[:, 128:]
            acc[...] += dot(group, table[kind])
            return carry

        lax.fori_loop(0, span, spread_out, 0, unroll=True)
    local = acc[...].astype(BF)
    for c in range(8):
        out = dot(local, l2l_ref[c])
        at = pl.ds(received * kinds + c * cells, cells)
        z_low[at, :] = out[:, :128]
        z_high[at, :] = out[:, 128:]
    for copy in copies:
        copy.wait()
    per = leaves // target.shape[0]

    def body(group, carry):
        first = group * 32

        def add_rows(u):
            for v in range(per):
                leaf = first * per + u * per + v
                lows, highs = [None] * 4, [None] * 4
                for j in range(entries):
                    at = pl.ds(far_ref[j * leaves + leaf], 1)
                    low, high = z_low[at, :], z_high[at, :]
                    k = j % 4
                    lows[k] = low if lows[k] is None else lows[k] + low
                    highs[k] = high if highs[k] is None else highs[k] + high
                at = pl.ds(leaf, 1)
                rows_low[at, :] = (lows[0] + lows[1]) + (lows[2] + lows[3])
                rows_high[at, :] = (highs[0] + highs[1]) + (highs[2] + highs[3])

        own = (offset_ref, dir_ref, scale_ref, add_ref, target, window, near_ref)
        near_leaves(begin, first, 32, own, add_rows)
        return carry

    lax.fori_loop(0, target.shape[0] // 32, body, 0)
    out_ref[:, :128] = rows_low[...].astype(BF)
    out_ref[:, 128:] = rows_high[...].astype(BF)


def far_kernel(counts_ref, tile_ref, exp_ref, dens_ref, *refs):
    near_refs, out_ref = refs[:-1], refs[-1]
    step = pl.program_id(0)
    leaves = out_ref.shape[0]
    unroll = 16
    lane = lax.broadcasted_iota(jnp.int32, (unroll, 128), 1)
    row = lax.broadcasted_iota(jnp.int32, (unroll, 128), 0)
    for group in range(leaves // unroll):
        at = pl.ds(group * unroll, unroll)
        out = dot(exp_ref[at, :], tile_ref[:, group * unroll * 128 : (group + 1) * unroll * 128])
        far = jnp.zeros((unroll, 128), F32)
        for u in range(unroll):
            far = jnp.where(row == u, out[:, u * 128 : (u + 1) * 128], far)
        near, begin = None, 0
        for ref in near_refs:
            at_near = jnp.clip(step * leaves + group * unroll - begin, 0, ref.shape[0] - unroll)
            part = ref[pl.ds(pl.multiple_of(at_near, unroll), unroll), :]
            near = part if near is None else jnp.where(step * leaves >= begin, part, near)
            begin += ref.shape[0]
        value = 0.5 * dens_ref[at, :] + near + far * (1.0 / math.sqrt(256))
        counts = spread(counts_ref, step * leaves + group * unroll, unroll)
        out_ref[at, :] = jnp.where(lane < counts, value, 0.0)


def params(mib=56):
    return pltpu.CompilerParams(vmem_limit_bytes=mib * 2**20)


def local(
    density, positions, counts, leaf_parent, child_pos, send_slots, far_source, far_type,
    near_offset, near_dir, coarse_source, coarse_type, m2l, m2m, l2l,
):
    leaves, panels = density.shape
    width = m2l.shape[1]
    kinds = m2l.shape[0]
    cells = coarse_source.shape[0]
    oct_size, leaf_size = lax.axis_size("oct"), lax.axis_size("leaf")
    group, place = lax.axis_index("oct"), lax.axis_index("leaf")
    cap = send_slots.shape[2]
    planes = positions.transpose(1, 0, 2)
    checks = check_rows(width)
    scale, add = shift_rows()

    code = (child_pos * cells + leaf_parent)[None, :]

    steps = 8
    block = leaves // steps
    chunk = leaves // 8
    target, source, tile, first, last, *send = pl.pallas_call(
        functools.partial(moments_kernel, (oct_size, leaf_size)),
        grid=(steps,),
        in_specs=[
            SMEM, SMEM,
            pl.BlockSpec((3, block, panels), lambda i: (0, i, 0)),
            pl.BlockSpec((block, panels), lambda i: (i, 0)),
            VMEM, VMEM, VMEM,
        ],
        out_specs=[
            pl.BlockSpec((block, ROWS, panels), lambda i: (i, 0, 0)),
            pl.BlockSpec((block, ROWS, panels), lambda i: (i, 0, 0)),
            pl.BlockSpec((width, block * panels), lambda i: (0, i)),
        ]
        + [VMEM] * 11,
        out_shape=[
            jax.ShapeDtypeStruct((leaves, ROWS, panels), BF),
            jax.ShapeDtypeStruct((leaves, ROWS, panels), BF),
            jax.ShapeDtypeStruct((width, leaves * panels), BF),
        ]
        + [jax.ShapeDtypeStruct((HW, ROWS, panels), BF)] * 2
        + [jax.ShapeDtypeStruct((cells + cap, width), BF)] * 2
        + [jax.ShapeDtypeStruct((cap, width), BF)] * 6
        + [jax.ShapeDtypeStruct((cells, width), BF)],
        scratch_shapes=[
            pltpu.VMEM((block, 128), F32),
            pltpu.VMEM((leaves, 128), F32),
            pltpu.VMEM((leaves, 128), F32),
            pltpu.VMEM((8 * PITCH, panels), F32),
            pltpu.VMEM((8 * PITCH, panels), F32),
        ],
        compiler_params=params(),
        name="moments",
    )(send_slots[0].T, counts, planes, density, code, checks.T, m2m)

    offsets = near_offset.T
    ways = near_dir.T

    spaces = [SMEM, SMEM, VMEM, VMEM, pl.BlockSpec(memory_space=pl.ANY)]

    def near_part(begin):
        parts = [before, source] if begin == 0 else [source]
        return pl.pallas_call(
            functools.partial(near_kernel, begin),
            in_specs=spaces + [pl.BlockSpec(memory_space=pl.ANY)] * len(parts),
            out_specs=VMEM,
            out_shape=jax.ShapeDtypeStruct((chunk, panels), F32),
            scratch_shapes=[
                pltpu.VMEM((chunk, ROWS, panels), BF),
                pltpu.VMEM((chunk + 2 * HW, ROWS, panels), BF),
                pltpu.SemaphoreType.DMA((3,)),
            ],
            compiler_params=params(),
            cost_estimate=pl.CostEstimate(
                flops=10**10, bytes_accessed=10**6, transcendentals=chunk * 2 * 65536
            ),
            name="near",
        )(offsets, ways, scale, add, target, *parts)

    def shifted(value, axis, by):
        size = lax.axis_size(axis)
        return lax.ppermute(value, axis, [(i, (i + by) % size) for i in range(size)])

    def moved(value, by):
        pairs = [(i, i + by) for i in range(leaf_size) if 0 <= i + by < leaf_size]
        return lax.ppermute(value, "leaf", pairs)

    def added(pieces):
        total = pieces[0].astype(F32)
        for piece in pieces[1:]:
            total = total + piece.astype(F32)
        return total.astype(BF)

    partial = send[8]
    by_two = shifted(send[0], "leaf", 2)
    by_one = shifted(send[1], "leaf", 1)
    by_three = shifted(partial, "leaf", 3)
    before, after = moved(last, 1), moved(first, -1)
    near = [None] * 4
    near[1] = near_part(chunk)
    near[1], by_one, by_two, by_three, before, after = lax.optimization_barrier(
        (near[1], by_one, by_two, by_three, before, after)
    )
    four = added([partial, by_one[:cells], by_two[:cells], by_three])
    strides = [shifted(four, "leaf", by) for by in (4, 8, 12)]
    back_one, back_two = moved(send[3], -1), moved(send[4], -2)
    four, source, target = lax.optimization_barrier((four, source, target))
    near[0] = near_part(0)
    near[0], four, back_one, back_two, *strides = lax.optimization_barrier(
        (near[0], four, back_one, back_two, *strides)
    )
    total = added([four, *strides])
    lower = shifted(total, "oct", 1)
    across = [
        shifted(send[5], "oct", -1), shifted(send[6], "oct", 1),
        shifted(send[7], "oct", oct_size // 2),
    ]
    total, source, target = lax.optimization_barrier((total, source, target))
    near[2] = near_part(2 * chunk)
    near[2], total, lower, *across = lax.optimization_barrier((near[2], total, lower, *across))
    pair = jnp.concatenate([total, lower], axis=0)
    pairs = [shifted(pair, "oct", by) for by in (2, 4, 6)]
    pair, source, target = lax.optimization_barrier((pair, source, target))
    near[3] = near_part(3 * chunk)
    near[3], pair, *pairs = lax.optimization_barrier((near[3], pair, *pairs))
    every_parent = [pair, *pairs]
    received = [by_two, by_one, send[2], back_one, back_two, *across]

    owner, slot = far_source // cap, far_source % cap
    owner_group, owner_place = owner // leaf_size, owner % leaf_size
    partner = jnp.where(
        owner_group == group,
        owner_place - place + 2,
        jnp.where(
            owner_group == (group + 1) % oct_size,
            5,
            jnp.where(owner_group == (group + oct_size - 1) % oct_size, 6, 7),
        ),
    )
    far_rows = (far_type * 8 + partner) * cap + slot
    own_row = kinds * 8 * cap + child_pos * cells + leaf_parent
    far_rows = jnp.concatenate([far_rows.T.reshape(-1), own_row])
    rest = leaves - 4 * chunk
    any_space = pl.BlockSpec(memory_space=pl.ANY)
    last_near, expansions = pl.pallas_call(
        functools.partial(translate_kernel, 4 * chunk),
        in_specs=[SMEM] * 5 + [VMEM] * 3 + [any_space] * 4 + [VMEM] * 12,
        out_specs=[VMEM, VMEM],
        out_shape=[
            jax.ShapeDtypeStruct((rest, panels), F32),
            jax.ShapeDtypeStruct((leaves, width), BF),
        ],
        scratch_shapes=[
            pltpu.VMEM((kinds * 8 * cap + 8 * cells, 128), F32),
            pltpu.VMEM((kinds * 8 * cap + 8 * cells, 128), F32),
            pltpu.VMEM((kinds * cells, 128), F32),
            pltpu.VMEM((kinds * cells, 128), F32),
            pltpu.VMEM((oct_size * cells, 128), F32),
            pltpu.VMEM((oct_size * cells, 128), F32),
            pltpu.VMEM((cells, width), F32),
            pltpu.VMEM((leaves, 128), F32),
            pltpu.VMEM((leaves, 128), F32),
            pltpu.VMEM((8 * cap, width), BF),
            pltpu.VMEM((rest, ROWS, panels), BF),
            pltpu.VMEM((rest + 2 * HW, ROWS, panels), BF),
            pltpu.VMEM(m2l.shape, BF),
            pltpu.SemaphoreType.DMA((3,)),
            pltpu.SemaphoreType.DMA((8,)),
        ],
        compiler_params=params(),
        name="translate",
    )(
        offsets, ways, far_rows, coarse_source.T, coarse_type.T, scale, add, l2l,
        target, source, after, m2l, *received, *every_parent,
    )
    near.append(last_near)

    return pl.pallas_call(
        far_kernel,
        grid=(steps,),
        in_specs=[
            SMEM,
            pl.BlockSpec((width, block * panels), lambda i: (0, i)),
            pl.BlockSpec((block, width), lambda i: (i, 0)),
            pl.BlockSpec((block, panels), lambda i: (i, 0)),
        ]
        + [VMEM] * len(near),
        out_specs=pl.BlockSpec((block, panels), lambda i: (i, 0)),
        out_shape=jax.ShapeDtypeStruct((leaves, panels), F32),
        compiler_params=params(),
        name="far",
    )(counts, tile, expansions, density, *near)


def solution(mesh):
    both = ("oct", "leaf")
    placed = (
        P(both, None), P(both, None, None), P(both), P(both), P(both), P(both, None, None),
        P(both, None), P(both, None), P(both, None), P(both, None),
        P("oct", None), P("oct", None), P(), P(), P(),
    )
    return jax.shard_map(
        local, mesh=mesh, in_specs=placed, out_specs=P(both, None), check_vma=False
    )
```

```python
import functools
import math

import jax
import jax.numpy as jnp
import ml_dtypes
import numpy as np
from jax import lax
from jax.experimental import pallas as pl
from jax.experimental.pallas import tpu as pltpu
from jax.sharding import PartitionSpec as P

HW = 32
KAPPA = 0.25
DELTA = 0.05
RADIUS = 2.0
RATE = -KAPPA * math.log2(math.e)
ROWS = 32
PITCH = 36
BF = jnp.bfloat16
F32 = jnp.float32
VMEM = pl.BlockSpec(memory_space=pltpu.VMEM)
SMEM = pl.BlockSpec(memory_space=pltpu.SMEM)


def np_split(values, number):
    pieces = []
    rest = values.astype(np.float32)
    for _ in range(number):
        piece = rest.astype(ml_dtypes.bfloat16)
        pieces.append(piece)
        rest = rest - piece.astype(np.float32)
    return pieces


def check_rows(number):
    middle = np.arange(number, dtype=np.float32) + np.float32(0.5)
    height = (1.0 - 2.0 * middle / np.float32(number)).astype(np.float32)
    radial = np.sqrt(np.maximum(1.0 - height * height, 0.0)).astype(np.float32)
    azimuth = np.float32(math.pi * (1.0 + math.sqrt(5.0))) * middle
    points = RADIUS * np.stack([radial * np.cos(azimuth), radial * np.sin(azimuth), height])
    high, low = np_split(points, 2)
    high, low = high.astype(np.float32), low.astype(np.float32)
    rounded = high + low
    squares = np_split(np.sum(rounded * rounded, axis=0), 3)
    rows = np.zeros((ROWS, number), np.float32)
    rows[0:3], rows[3:6], rows[6:9], rows[9:12] = -2 * high, -2 * low, -2 * high, -2 * low
    for k in range(3):
        rows[12 + k] = squares[k].astype(np.float32)
    rows[15:18] = 1.0
    return rows.astype(ml_dtypes.bfloat16)


def shift_rows():
    scale = np.zeros((27, ROWS, 128), np.float32)
    add = np.zeros((27, ROWS, 128), np.float32)
    scale[:, 0:18] = 1.0
    scale[:, 31] = 1.0
    for d in range(27):
        shift = 2.0 * np.array([d // 9 - 1, d // 3 % 3 - 1, d % 3 - 1], np.float32)
        for k in range(3):
            scale[d, 18 + k] = -shift[k]
            scale[d, 21 + k] = -shift[k]
            add[d, 24 + k] = -2 * shift[k]
            add[d, 27 + k] = -2 * shift[k]
        add[d, 30] = np.sum(shift * shift)
    return scale.astype(ml_dtypes.bfloat16), add.astype(ml_dtypes.bfloat16)


def split(value):
    high = value.astype(BF).astype(F32)
    return high, value - high


def panel_rows(coords, weights):
    highs, lows, square = [], [], None
    for value in coords:
        high, rest = split(value)
        low = rest.astype(BF).astype(F32)
        highs.append(high)
        lows.append(low)
        rounded = high + low
        square = rounded * rounded if square is None else square + rounded * rounded
    one = jnp.ones_like(square)
    zero = jnp.zeros_like(square)

    def thirds(value):
        first, rest = split(value)
        second, rest = split(rest)
        return [first, second, rest]

    minus_high = [-2.0 * value for value in highs]
    minus_low = [-2.0 * value for value in lows]
    target = highs + highs + lows + lows + [one] * 3 + thirds(square + DELTA * DELTA)
    target += [one] * 6 + highs + lows + [one, zero]
    source = minus_high + minus_low + minus_high + minus_low + thirds(square) + [one] * 3
    source += minus_high + minus_low + [zero] * 7 + [weights]
    return target, source


def spread(ref, first, number):
    row = lax.broadcasted_iota(jnp.int32, (number, 128), 0)
    value = jnp.full((number, 128), ref[first], jnp.int32)
    for u in range(1, number):
        value = jnp.where(row == u, ref[first + u], value)
    return value


def place_rows(rows, scratch, write):
    for r, value in enumerate(rows):
        scratch[pl.ds(r, 8, stride=PITCH), :] = value
    for u in range(8):
        write(u, scratch[u * PITCH : u * PITCH + ROWS, :].astype(BF))


def green(squared):
    low = squared.astype(BF)
    inverse = lax.rsqrt(low)
    return jnp.exp2((low * inverse) * BF(RATE)) * inverse


def dot(a, b, over=((1,), (0,))):
    return lax.dot_general(a, b, (over, ((), ())), preferred_element_type=F32)


def moments_kernel(
    sizes, slots_ref, counts_ref, pos_ref, dens_ref, code_ref, checks_ref, m2m_ref,
    target_ref, source_ref, tile_ref, *rest,
):
    send_refs, part_refs = rest[:8], ((rest[8], 0), (rest[0], 0), (rest[1], HW))
    weights, moments_low, moments_high, scratch, spare = rest[9:]
    step = pl.program_id(0)
    leaves = pos_ref.shape[1]
    total = moments_low.shape[0]
    checks = checks_ref[...]
    lane = lax.broadcasted_iota(jnp.int32, (8, 128), 1)

    def build(group, carry):
        at = pl.ds(pl.multiple_of(group * 8, 8), 8)
        masked = jnp.where(lane < spread(counts_ref, step * leaves + group * 8, 8), dens_ref[at, :], 0.0)
        weights[at, :] = masked
        target, source = panel_rows([pos_ref[d, at, :] for d in range(3)], masked)

        def put_target(u, value):
            target_ref[group * 8 + u] = value

        def put_source(u, value):
            source_ref[group * 8 + u] = value

        place_rows(target, scratch, put_target)
        place_rows(source, spare, put_source)
        return carry

    lax.fori_loop(0, leaves // 8, build, 0)
    row = lax.broadcasted_iota(jnp.int32, (16, 128), 0)

    def squares(leaf):
        return dot(checks, jnp.concatenate([target_ref[leaf + u] for u in range(4)], axis=1))

    def finish(first, part, kernel, sums):
        pair = first // 2 + part * 2
        tile_ref[pair], tile_ref[pair + 1] = kernel[:, :256], kernel[:, 256:]
        block = part // 4
        value = weights[pl.ds(pl.multiple_of(first + block * 16, 16), 16), :]
        apart = [jnp.where(row == part % 4 * 4 + u, value, 0.0) for u in range(4)]
        out = dot(jnp.concatenate(apart, axis=1).astype(BF), kernel, ((1,), (1,)))
        sums[block] = out if part % 4 == 0 else sums[block] + out
        if part % 4 == 3:
            low = (sums[block] * (1.0 / math.sqrt(128))).astype(BF).astype(F32)
            at = pl.ds(pl.multiple_of(step * leaves + first + block * 16, 16), 16)
            moments_low[at, :], moments_high[at, :] = low[:, :128], low[:, 128:]

    def expand(group, carry):
        first = group * span
        ahead, kernels, sums = {}, {}, {}
        for s in range(span // 4 + 2):
            if s < span // 4:
                ahead[s] = squares(first + s * 4)
            if 0 <= s - 1 < span // 4:
                kernels[s - 1] = green(ahead.pop(s - 1))
            if 0 <= s - 2:
                finish(first, s - 2, kernels.pop(s - 2), sums)
        return carry

    span = 64
    lax.fori_loop(0, leaves // span, expand, 0)

    @pl.when(step == 0)
    def _():
        send_refs[3][0:HW] = source_ref[0:HW]

    @pl.when(step == pl.num_programs(0) - 1)
    def _():
        send_refs[1][0:HW] = source_ref[leaves - HW :]
        group, place = lax.axis_index("oct"), lax.axis_index("leaf")
        oct_size, leaf_size = sizes
        for partner in range(8):
            if partner < 5:
                other = jnp.clip(place + 2 - partner, 0, leaf_size - 1)
                other = group * leaf_size + other
            else:
                by = (oct_size - 1, 1, oct_size // 2)[partner - 5]
                other = lax.rem(group + by, oct_size) * leaf_size + place

            def pick(s, carry):
                slot = jnp.maximum(slots_ref[s, other], 0)
                spare[pl.ds(s, 1), :] = moments_low[pl.ds(slot, 1), :]
                scratch[pl.ds(s, 1), :] = moments_high[pl.ds(slot, 1), :]
                return carry

            lax.fori_loop(0, 32, pick, 0, unroll=8)
            last = send_refs[partner].shape[0]
            send_refs[partner][last - 2] = spare[0:32, :].astype(BF)
            send_refs[partner][last - 1] = scratch[0:32, :].astype(BF)
        low = jnp.concatenate([moments_low[...], moments_high[...]], axis=1).astype(BF)
        parents = 64
        acc = jnp.zeros((parents, 2 * 128), F32)
        for c in range(8):
            row = lax.broadcasted_iota(jnp.int32, (parents, total), 0) + c * parents
            chosen = jnp.where(row == code_ref[...], 1.0, 0.0).astype(BF)
            high, rest = split(dot(chosen, low))
            acc += dot(high.astype(BF), m2m_ref[c]) + dot(rest.astype(BF), m2m_ref[c])
        for part_ref, at in part_refs:
            for k in range(4):
                piece = acc[k % 2 * 32 : k % 2 * 32 + 32, k // 2 * 128 : k // 2 * 128 + 128]
                part_ref[at + k] = piece.astype(BF)


def load_window(begin, target_ref, parts, target, window, sems):
    leaves = target.shape[0]
    copies = [pltpu.make_async_copy(target_ref.at[begin : begin + leaves], target, sems.at[2])]
    at = 0
    for k, part in enumerate(parts):
        size = part.shape[0]
        if size < 64:
            size, part = HW, part.at[0:HW]
        if part.shape[0] >= 64:
            low = max(begin - HW, 0)
            size = min(begin + leaves + HW, size) - low
            part = part.at[low : low + size]
        copies.append(pltpu.make_async_copy(part, window.at[at : at + size], sems.at[k]))
        at += size
    for copy in copies:
        copy.start()
    return copies


def near_leaves(begin, first, number, refs, beside=None):
    offset_ref, dir_ref, scale_ref, add_ref, target, window, out_ref = refs

    def squares(leaf):
        whole = begin + leaf
        rows, weights = [], []
        for j in range(4):
            base = window[leaf + HW + offset_ref[j, whole]]
            way = dir_ref[j, whole]
            rows.append(base * scale_ref[way] + add_ref[way])
            weights.append(base[16:32])
        value = dot(target[leaf], jnp.concatenate(rows, 1), ((0,), (0,)))
        return value, jnp.concatenate(weights, 1)

    depth = 2
    ahead = []
    for u in range(number + depth):
        if u < number:
            ahead.append(squares(first + u))
            if beside is not None:
                beside(u)
        if u >= depth:
            value, weights = ahead[u - depth]
            ahead[u - depth] = None
            out = dot(weights, green(value), ((1,), (1,)))[15:16]
            out_ref[pl.ds(first + u - depth, 1), :] = out * (1.0 / math.sqrt(512))


def near_kernel(begin, offset_ref, dir_ref, scale_ref, add_ref, target_ref, *refs):
    *parts, out_ref, target, window, sems = refs
    for copy in load_window(begin, target_ref, parts, target, window, sems):
        copy.wait()

    def body(group, carry):
        own = (offset_ref, dir_ref, scale_ref, add_ref, target, window, out_ref)
        near_leaves(begin, group * 32, 32, own)
        return carry

    lax.fori_loop(0, target.shape[0] // 32, body, 0)


def translate_kernel(
    begin, offset_ref, dir_ref, far_ref, coarse_from_ref, coarse_to_ref,
    scale_ref, add_ref, l2l_ref, target_ref, source_ref, after_ref, m2l_ref, *refs,
):
    recv_refs, parent_refs = refs[:8], refs[8:12]
    counts_ref, tile_ref, dens_ref, *near_refs, out_ref = refs[12:20]
    z_low, z_high, groups_low, groups_high, parents_low, parents_high = refs[20:26]
    acc, rows_low, rows_high, recv_ref, target, window, near_ref, table, *every_sem = refs[26:]
    sems, table_sems, tile_sems = every_sem
    pieces = table_sems.shape[0]
    kinds = m2l_ref.shape[0]
    span = kinds // pieces
    received = recv_ref.shape[0]
    cells = acc.shape[0]
    leaves = rows_low.shape[0]
    entries = far_ref.shape[0] // leaves
    coarse, _ = coarse_from_ref.shape

    loads = [
        pltpu.make_async_copy(
            m2l_ref.at[k * span : (k + 1) * span], table.at[k * span : (k + 1) * span],
            table_sems.at[k],
        )
        for k in range(pieces)
    ]
    for load in loads:
        load.start()
    copies = load_window(begin, target_ref, [source_ref, after_ref], target, window, sems)
    groups_low[...] = jnp.zeros(groups_low.shape, F32)
    groups_high[...] = jnp.zeros(groups_high.shape, F32)
    acc[...] = jnp.zeros(acc.shape, F32)
    oct_size = parents_low.shape[0] // cells
    before = 0
    for part in parent_refs:
        for k in range(2):
            owner = lax.rem(lax.axis_index("oct") + oct_size - before, oct_size)
            at = pl.ds(pl.multiple_of(owner * cells, cells), cells)
            piece = part[k * 4 : k * 4 + 4].astype(F32)
            parents_low[at, :] = piece[0:2].reshape(cells, 128)
            parents_high[at, :] = piece[2:4].reshape(cells, 128)
            before += 1
    for k, part in enumerate(recv_refs):
        last = part.shape[0]
        recv_ref[k * 32 : (k + 1) * 32, :128] = part[last - 2]
        recv_ref[k * 32 : (k + 1) * 32, 128:] = part[last - 1]

    def gather(q, carry):
        for j in range(coarse):
            at = pl.ds(coarse_to_ref[j, q] * cells + q, 1)
            row = pl.ds(coarse_from_ref[j, q], 1)
            groups_low[at, :] = groups_low[at, :] + parents_low[row, :]
            groups_high[at, :] = groups_high[at, :] + parents_high[row, :]
        return carry

    lax.fori_loop(0, cells, gather, 0)
    tile_blocks, width = tile_ref.shape[0] // 32, 32
    slots = [kinds + width * k for k in range(tile_blocks - 3)] + [0, width, kinds]
    tiles = [
        pltpu.make_async_copy(
            tile_ref.at[k * width : (k + 1) * width], table.at[slots[k] : slots[k] + width],
            tile_sems.at[k],
        )
        for k in range(tile_blocks)
    ]
    for k in range(tile_blocks - 3):
        tiles[k].start()
    for k in range(pieces):
        loads[k].wait()

        def spread_out(t, carry):
            kind = k * span + t
            at = pl.ds(pl.multiple_of(kind * cells, cells), cells)
            group = jnp.concatenate([groups_low[at, :], groups_high[at, :]], axis=1).astype(BF)
            out = dot(recv_ref[...], table[kind])
            at = pl.ds(pl.multiple_of(kind * received, received), received)
            z_low[at, :] = out[:, :128]
            z_high[at, :] = out[:, 128:]
            acc[...] += dot(group, table[kind])
            return carry

        lax.fori_loop(0, span, spread_out, 0, unroll=True)
    for k in range(tile_blocks - 3, tile_blocks - 1):
        tiles[k].start()
    local = acc[...].astype(BF)
    for c in range(8):
        out = dot(local, l2l_ref[c])
        at = pl.ds(received * kinds + c * cells, cells)
        z_low[at, :] = out[:, :128]
        z_high[at, :] = out[:, 128:]
    for copy in copies:
        copy.wait()
    per = leaves // target.shape[0]

    def body(group, carry):
        first = group * 32

        def add_rows(u):
            for v in range(per):
                leaf = first * per + u * per + v
                lows, highs = [None] * 4, [None] * 4
                for j in range(entries):
                    at = pl.ds(far_ref[j * leaves + leaf], 1)
                    low, high = z_low[at, :], z_high[at, :]
                    k = j % 4
                    lows[k] = low if lows[k] is None else lows[k] + low
                    highs[k] = high if highs[k] is None else highs[k] + high
                at = pl.ds(leaf, 1)
                rows_low[at, :] = (lows[0] + lows[1]) + (lows[2] + lows[3])
                rows_high[at, :] = (highs[0] + highs[1]) + (highs[2] + highs[3])

        own = (offset_ref, dir_ref, scale_ref, add_ref, target, window, near_ref)
        near_leaves(begin, first, 32, own, add_rows)
        return carry

    lax.fori_loop(0, target.shape[0] // 32, body, 0)
    row = lax.broadcasted_iota(jnp.int32, (16, 128), 0)
    lane = lax.broadcasted_iota(jnp.int32, (16, 128), 1)
    for k in range(tile_blocks):
        tiles[k].wait()
        near_part = near_refs[k] if k < len(near_refs) else near_ref
        near_first = 0 if k < len(near_refs) else k * 2 * width - begin

        def far(group, carry):
            first = k * 2 * width + group * 16
            at = pl.ds(pl.multiple_of(first, 16), 16)
            local = jnp.concatenate([rows_low[at, :], rows_high[at, :]], axis=1).astype(BF)
            value = jnp.zeros((16, 128), F32)
            for u in range(8):
                out = dot(local, table[slots[k] + group * 8 + u])
                value = jnp.where(row == 2 * u, out[:, :128], value)
                value = jnp.where(row == 2 * u + 1, out[:, 128:], value)
            near = near_part[pl.ds(pl.multiple_of(near_first + group * 16, 16), 16), :]
            total = 0.5 * dens_ref[at, :] + near + value * (1.0 / math.sqrt(256))
            out_ref[at, :] = jnp.where(lane < spread(counts_ref, first, 16), total, 0.0)
            return carry

        lax.fori_loop(0, width // 8, far, 0)
        if k == 0:
            tiles[tile_blocks - 1].start()


def params(mib=56):
    return pltpu.CompilerParams(vmem_limit_bytes=mib * 2**20)


def local(
    density, positions, counts, leaf_parent, child_pos, send_slots, far_source, far_type,
    near_offset, near_dir, coarse_source, coarse_type, m2l, m2m, l2l,
):
    leaves, panels = density.shape
    width = m2l.shape[1]
    kinds = m2l.shape[0]
    cells = coarse_source.shape[0]
    oct_size, leaf_size = lax.axis_size("oct"), lax.axis_size("leaf")
    group, place = lax.axis_index("oct"), lax.axis_index("leaf")
    cap = send_slots.shape[2]
    planes = positions.transpose(1, 0, 2)
    checks = check_rows(width)
    scale, add = shift_rows()

    code = (child_pos * cells + leaf_parent)[None, :]

    steps = 8
    block = leaves // steps
    chunk = leaves // 8
    target, source, tile, *send = pl.pallas_call(
        functools.partial(moments_kernel, (oct_size, leaf_size)),
        grid=(steps,),
        in_specs=[
            SMEM, SMEM,
            pl.BlockSpec((3, block, panels), lambda i: (0, i, 0)),
            pl.BlockSpec((block, panels), lambda i: (i, 0)),
            VMEM, VMEM, VMEM,
        ],
        out_specs=[
            pl.BlockSpec((block, ROWS, panels), lambda i: (i, 0, 0)),
            pl.BlockSpec((block, ROWS, panels), lambda i: (i, 0, 0)),
            pl.BlockSpec((block // 2, width, 2 * panels), lambda i: (i, 0, 0)),
        ]
        + [VMEM] * 9,
        out_shape=[
            jax.ShapeDtypeStruct((leaves, ROWS, panels), BF),
            jax.ShapeDtypeStruct((leaves, ROWS, panels), BF),
            jax.ShapeDtypeStruct((leaves // 2, width, 2 * panels), BF),
        ]
        + [jax.ShapeDtypeStruct((n, 32, 128), BF) for n in (6, HW + 6, 2, HW + 2, 2, 2, 2, 2, 4)],
        scratch_shapes=[
            pltpu.VMEM((block, 128), F32),
            pltpu.VMEM((leaves, 128), F32),
            pltpu.VMEM((leaves, 128), F32),
            pltpu.VMEM((8 * PITCH, panels), F32),
            pltpu.VMEM((8 * PITCH, panels), F32),
        ],
        compiler_params=params(),
        name="moments",
    )(send_slots[0].T, counts, planes, density, code, checks.T, m2m)

    offsets = near_offset.T
    ways = near_dir.T

    spaces = [SMEM, SMEM, VMEM, VMEM, pl.BlockSpec(memory_space=pl.ANY)]

    def near_part(begin):
        parts = [before, source] if begin == 0 else [source]
        return pl.pallas_call(
            functools.partial(near_kernel, begin),
            in_specs=spaces + [pl.BlockSpec(memory_space=pl.ANY)] * len(parts),
            out_specs=VMEM,
            out_shape=jax.ShapeDtypeStruct((chunk, panels), F32),
            scratch_shapes=[
                pltpu.VMEM((chunk, ROWS, panels), BF),
                pltpu.VMEM((chunk + 2 * HW, ROWS, panels), BF),
                pltpu.SemaphoreType.DMA((3,)),
            ],
            compiler_params=params(),
            cost_estimate=pl.CostEstimate(
                flops=10**10, bytes_accessed=10**6, transcendentals=chunk * 2 * 65536
            ),
            name="near",
        )(offsets, ways, scale, add, target, *parts)

    def shifted(value, axis, by):
        size = lax.axis_size(axis)
        return lax.ppermute(value, axis, [(i, (i + by) % size) for i in range(size)])

    def added(pieces):
        total = pieces[0].astype(F32)
        for piece in pieces[1:]:
            total = total + piece.astype(F32)
        return total.astype(BF)

    partial = send[8]
    by_one = shifted(send[1], "leaf", 1)
    back_one = shifted(send[3], "leaf", -1)
    by_two = shifted(send[0], "leaf", 2)
    back_two = shifted(send[4], "leaf", -2)
    by_three = shifted(partial, "leaf", 3)
    near = [None] * 4
    near[1] = near_part(chunk)
    near[1], by_one, by_two, by_three, back_one, back_two = lax.optimization_barrier(
        (near[1], by_one, by_two, by_three, back_one, back_two)
    )
    before, after = by_one, back_one
    four = added([partial, by_one[HW : HW + 4], by_two[:4], by_three])
    strides = [shifted(four, "leaf", by) for by in (4, 8, 12)]
    upper = shifted(send[5], "oct", -1)
    four, source, target = lax.optimization_barrier((four, source, target))
    near[0] = near_part(0)
    near[0], four, upper, *strides = lax.optimization_barrier((near[0], four, upper, *strides))
    total = added([four, *strides])
    lower = shifted(jnp.concatenate([total, send[6]], axis=0), "oct", 1)
    total, source, target = lax.optimization_barrier((total, source, target))
    near[2] = near_part(2 * chunk)
    near[2], total, lower = lax.optimization_barrier((near[2], total, lower))
    pair = jnp.concatenate([total, lower[:4], send[7]], axis=0)
    pairs = [shifted(pair, "oct", by) for by in (2, 4, 6)]
    pair, source, target = lax.optimization_barrier((pair, source, target))
    near[3] = near_part(3 * chunk)
    near[3], pair, *pairs = lax.optimization_barrier((near[3], pair, *pairs))
    every_parent = [pair, *pairs]
    received = [by_two, by_one, send[2], back_one, back_two, upper, lower, pairs[1]]

    owner, slot = far_source // cap, far_source % cap
    owner_group, owner_place = owner // leaf_size, owner % leaf_size
    partner = jnp.where(
        owner_group == group,
        owner_place - place + 2,
        jnp.where(
            owner_group == (group + 1) % oct_size,
            5,
            jnp.where(owner_group == (group + oct_size - 1) % oct_size, 6, 7),
        ),
    )
    far_rows = (far_type * 8 + partner) * cap + slot
    own_row = kinds * 8 * cap + child_pos * cells + leaf_parent
    far_rows = jnp.concatenate([far_rows.T.reshape(-1), own_row])
    rest = leaves - 4 * chunk
    any_space = pl.BlockSpec(memory_space=pl.ANY)
    return pl.pallas_call(
        functools.partial(translate_kernel, 4 * chunk),
        in_specs=[SMEM] * 5 + [VMEM] * 3 + [any_space] * 4 + [VMEM] * 12
        + [SMEM, any_space] + [VMEM] * 5,
        out_specs=VMEM,
        out_shape=jax.ShapeDtypeStruct((leaves, panels), F32),
        scratch_shapes=[
            pltpu.VMEM((kinds * 8 * cap + 8 * cells, 128), F32),
            pltpu.VMEM((kinds * 8 * cap + 8 * cells, 128), F32),
            pltpu.VMEM((kinds * cells, 128), F32),
            pltpu.VMEM((kinds * cells, 128), F32),
            pltpu.VMEM((oct_size * cells, 128), F32),
            pltpu.VMEM((oct_size * cells, 128), F32),
            pltpu.VMEM((cells, width), F32),
            pltpu.VMEM((leaves, 128), F32),
            pltpu.VMEM((leaves, 128), F32),
            pltpu.VMEM((8 * cap, width), BF),
            pltpu.VMEM((rest, ROWS, panels), BF),
            pltpu.VMEM((rest + 2 * HW, ROWS, panels), BF),
            pltpu.VMEM((rest, panels), F32),
            pltpu.VMEM((kinds + 5 * 32, width, width), BF),
            pltpu.SemaphoreType.DMA((3,)),
            pltpu.SemaphoreType.DMA((8,)),
            pltpu.SemaphoreType.DMA((8,)),
        ],
        compiler_params=params(62),
        name="translate",
    )(
        offsets, ways, far_rows, coarse_source.T, coarse_type.T, scale, add, l2l,
        target, source, after, m2l, *received, *every_parent, counts, tile, density, *near,
    )


def solution(mesh):
    both = ("oct", "leaf")
    placed = (
        P(both, None), P(both, None, None), P(both), P(both), P(both), P(both, None, None),
        P(both, None), P(both, None), P(both, None), P(both, None),
        P("oct", None), P("oct", None), P(), P(), P(),
    )
    return jax.shard_map(
        local, mesh=mesh, in_specs=placed, out_specs=P(both, None), check_vma=False
    )
```

```python
import functools
import math

import jax
import jax.numpy as jnp
import ml_dtypes
import numpy as np
from jax import lax
from jax.experimental import pallas as pl
from jax.experimental.pallas import tpu as pltpu
from jax.sharding import PartitionSpec as P

HW = 32
KAPPA = 0.25
DELTA = 0.05
RADIUS = 2.0
RATE = -KAPPA * math.log2(math.e)
ROWS = 32
PITCH = 36
BF = jnp.bfloat16
F32 = jnp.float32
VMEM = pl.BlockSpec(memory_space=pltpu.VMEM)
SMEM = pl.BlockSpec(memory_space=pltpu.SMEM)


def np_split(values, number):
    pieces = []
    rest = values.astype(np.float32)
    for _ in range(number):
        piece = rest.astype(ml_dtypes.bfloat16)
        pieces.append(piece)
        rest = rest - piece.astype(np.float32)
    return pieces


def check_rows(number):
    middle = np.arange(number, dtype=np.float32) + np.float32(0.5)
    height = (1.0 - 2.0 * middle / np.float32(number)).astype(np.float32)
    radial = np.sqrt(np.maximum(1.0 - height * height, 0.0)).astype(np.float32)
    azimuth = np.float32(math.pi * (1.0 + math.sqrt(5.0))) * middle
    points = RADIUS * np.stack([radial * np.cos(azimuth), radial * np.sin(azimuth), height])
    high, low = np_split(points, 2)
    high, low = high.astype(np.float32), low.astype(np.float32)
    rounded = high + low
    squares = np_split(np.sum(rounded * rounded, axis=0), 3)
    rows = np.zeros((ROWS, number), np.float32)
    rows[0:3], rows[3:6], rows[6:9], rows[9:12] = -2 * high, -2 * low, -2 * high, -2 * low
    for k in range(3):
        rows[12 + k] = squares[k].astype(np.float32)
    rows[15:18] = 1.0
    return rows.astype(ml_dtypes.bfloat16)


def shift_rows():
    scale = np.zeros((27, ROWS, 128), np.float32)
    add = np.zeros((27, ROWS, 128), np.float32)
    scale[:, 0:18] = 1.0
    scale[:, 31] = 1.0
    for d in range(27):
        shift = 2.0 * np.array([d // 9 - 1, d // 3 % 3 - 1, d % 3 - 1], np.float32)
        for k in range(3):
            scale[d, 18 + k] = -shift[k]
            scale[d, 21 + k] = -shift[k]
            add[d, 24 + k] = -2 * shift[k]
            add[d, 27 + k] = -2 * shift[k]
        add[d, 30] = np.sum(shift * shift)
    return scale.astype(ml_dtypes.bfloat16), add.astype(ml_dtypes.bfloat16)


def split(value):
    high = value.astype(BF).astype(F32)
    return high, value - high


def panel_rows(coords, weights):
    highs, lows, square = [], [], None
    for value in coords:
        high, rest = split(value)
        low = rest.astype(BF).astype(F32)
        highs.append(high)
        lows.append(low)
        rounded = high + low
        square = rounded * rounded if square is None else square + rounded * rounded
    one = jnp.ones_like(square)
    zero = jnp.zeros_like(square)

    def thirds(value):
        first, rest = split(value)
        second, rest = split(rest)
        return [first, second, rest]

    minus_high = [-2.0 * value for value in highs]
    minus_low = [-2.0 * value for value in lows]
    target = highs + highs + lows + lows + [one] * 3 + thirds(square + DELTA * DELTA)
    target += [one] * 6 + highs + lows + [one, zero]
    source = minus_high + minus_low + minus_high + minus_low + thirds(square) + [one] * 3
    source += minus_high + minus_low + [zero] * 7 + [weights]
    return target, source


def spread(ref, first, number):
    row = lax.broadcasted_iota(jnp.int32, (number, 128), 0)
    value = jnp.full((number, 128), ref[first], jnp.int32)
    for u in range(1, number):
        value = jnp.where(row == u, ref[first + u], value)
    return value


def place_rows(rows, scratch, write):
    for r, value in enumerate(rows):
        scratch[pl.ds(r, 8, stride=PITCH), :] = value
    for u in range(8):
        write(u, scratch[u * PITCH : u * PITCH + ROWS, :].astype(BF))


def green(squared):
    low = squared.astype(BF)
    inverse = lax.rsqrt(low)
    return jnp.exp2((low * inverse) * BF(RATE)) * inverse


def dot(a, b, over=((1,), (0,))):
    return lax.dot_general(a, b, (over, ((), ())), preferred_element_type=F32)


def moments_kernel(
    sizes, slots_ref, counts_ref, pos_ref, dens_ref, code_ref, checks_ref, m2m_ref,
    target_ref, source_ref, tile_ref, *rest,
):
    send_refs, part_refs = rest[:8], ((rest[8], 0), (rest[0], 0), (rest[1], HW))
    weights, moments_low, moments_high, scratch, spare = rest[9:]
    step = pl.program_id(0)
    leaves = pos_ref.shape[1]
    total = moments_low.shape[0]
    checks = checks_ref[...]
    lane = lax.broadcasted_iota(jnp.int32, (8, 128), 1)

    def build(group, carry):
        at = pl.ds(pl.multiple_of(group * 8, 8), 8)
        masked = jnp.where(lane < spread(counts_ref, step * leaves + group * 8, 8), dens_ref[at, :], 0.0)
        weights[at, :] = masked
        target, source = panel_rows([pos_ref[d, at, :] for d in range(3)], masked)

        def put_target(u, value):
            target_ref[group * 8 + u] = value

        def put_source(u, value):
            source_ref[group * 8 + u] = value

        place_rows(target, scratch, put_target)
        place_rows(source, spare, put_source)
        return carry

    lax.fori_loop(0, leaves // 8, build, 0)
    row = lax.broadcasted_iota(jnp.int32, (16, 128), 0)

    def squares(leaf):
        return dot(checks, jnp.concatenate([target_ref[leaf + u] for u in range(2)], axis=1))

    def finish(first, part, kernel, sums):
        tile_ref[first // 2 + part] = kernel
        block = part // 8
        value = weights[pl.ds(pl.multiple_of(first + block * 16, 16), 16), :]
        apart = [jnp.where(row == part % 8 * 2 + u, value, 0.0) for u in range(2)]
        out = dot(jnp.concatenate(apart, axis=1).astype(BF), kernel, ((1,), (1,)))
        sums[block] = out if part % 8 == 0 else sums[block] + out
        if part % 8 == 7:
            low = (sums[block] * (1.0 / math.sqrt(128))).astype(BF).astype(F32)
            at = pl.ds(pl.multiple_of(step * leaves + first + block * 16, 16), 16)
            moments_low[at, :], moments_high[at, :] = low[:, :128], low[:, 128:]

    def expand(group, carry):
        first = group * span
        ahead, kernels, sums = {}, {}, {}
        for s in range(span // 2 + 4):
            if s < span // 2:
                ahead[s] = squares(first + s * 2)
            if 0 <= s - 2 < span // 2:
                kernels[s - 2] = green(ahead.pop(s - 2))
            if 0 <= s - 4:
                finish(first, s - 4, kernels.pop(s - 4), sums)
        return carry

    span = 64
    lax.fori_loop(0, leaves // span, expand, 0)

    @pl.when(step == 0)
    def _():
        send_refs[3][0:HW] = source_ref[0:HW]

    @pl.when(step == pl.num_programs(0) - 1)
    def _():
        send_refs[1][0:HW] = source_ref[leaves - HW :]
        group, place = lax.axis_index("oct"), lax.axis_index("leaf")
        oct_size, leaf_size = sizes
        for partner in range(8):
            if partner < 5:
                other = jnp.clip(place + 2 - partner, 0, leaf_size - 1)
                other = group * leaf_size + other
            else:
                by = (oct_size - 1, 1, oct_size // 2)[partner - 5]
                other = lax.rem(group + by, oct_size) * leaf_size + place

            def pick(s, carry):
                slot = jnp.maximum(slots_ref[s, other], 0)
                spare[pl.ds(s, 1), :] = moments_low[pl.ds(slot, 1), :]
                scratch[pl.ds(s, 1), :] = moments_high[pl.ds(slot, 1), :]
                return carry

            lax.fori_loop(0, 32, pick, 0, unroll=8)
            last = send_refs[partner].shape[0]
            send_refs[partner][last - 2] = spare[0:32, :].astype(BF)
            send_refs[partner][last - 1] = scratch[0:32, :].astype(BF)
        low = jnp.concatenate([moments_low[...], moments_high[...]], axis=1).astype(BF)
        parents = 64
        acc = jnp.zeros((parents, 2 * 128), F32)
        for c in range(8):
            row = lax.broadcasted_iota(jnp.int32, (parents, total), 0) + c * parents
            chosen = jnp.where(row == code_ref[...], 1.0, 0.0).astype(BF)
            high, rest = split(dot(chosen, low))
            acc += dot(high.astype(BF), m2m_ref[c]) + dot(rest.astype(BF), m2m_ref[c])
        for part_ref, at in part_refs:
            for k in range(4):
                piece = acc[k % 2 * 32 : k % 2 * 32 + 32, k // 2 * 128 : k // 2 * 128 + 128]
                part_ref[at + k] = piece.astype(BF)


def load_window(begin, target_ref, parts, target, window, sems):
    leaves = target.shape[0]
    copies = [pltpu.make_async_copy(target_ref.at[begin : begin + leaves], target, sems.at[2])]
    at = 0
    for k, part in enumerate(parts):
        size = part.shape[0]
        if size < 64:
            size, part = HW, part.at[0:HW]
        if part.shape[0] >= 64:
            low = max(begin - HW, 0)
            size = min(begin + leaves + HW, size) - low
            part = part.at[low : low + size]
        copies.append(pltpu.make_async_copy(part, window.at[at : at + size], sems.at[k]))
        at += size
    for copy in copies:
        copy.start()
    return copies


def near_leaves(begin, first, number, refs, beside=None):
    offset_ref, dir_ref, scale_ref, add_ref, target, window, out_ref = refs

    def squares(leaf):
        whole = begin + leaf
        rows, weights = [], []
        for j in range(4):
            base = window[leaf + HW + offset_ref[j, whole]]
            way = dir_ref[j, whole]
            rows.append(base * scale_ref[way] + add_ref[way])
            weights.append(base[16:32])
        value = dot(target[leaf], jnp.concatenate(rows, 1), ((0,), (0,)))
        return value, jnp.concatenate(weights, 1)

    depth = 2
    ahead = []
    for u in range(number + depth):
        if u < number:
            ahead.append(squares(first + u))
            if beside is not None:
                beside(u)
        if u >= depth:
            value, weights = ahead[u - depth]
            ahead[u - depth] = None
            out = dot(weights, green(value), ((1,), (1,)))[15:16]
            out_ref[pl.ds(first + u - depth, 1), :] = out * (1.0 / math.sqrt(512))


def near_kernel(begin, offset_ref, dir_ref, scale_ref, add_ref, target_ref, *refs):
    *parts, out_ref, target, window, sems = refs
    for copy in load_window(begin, target_ref, parts, target, window, sems):
        copy.wait()

    def body(group, carry):
        own = (offset_ref, dir_ref, scale_ref, add_ref, target, window, out_ref)
        near_leaves(begin, group * 64, 64, own)
        return carry

    lax.fori_loop(0, target.shape[0] // 64, body, 0)


def translate_kernel(
    begin, offset_ref, dir_ref, far_ref, coarse_from_ref, coarse_to_ref,
    scale_ref, add_ref, l2l_ref, target_ref, source_ref, after_ref, m2l_ref, *refs,
):
    recv_refs, parent_refs = refs[:8], refs[8:12]
    counts_ref, tile_ref, dens_ref, *near_refs, out_ref = refs[12:20]
    z, groups_low, groups_high, parents_low, parents_high = refs[20:25]
    acc, rows_low, rows_high, recv_ref, target, window, near_ref, table, *every_sem = refs[25:]
    second = z.shape[0] // 2
    sems, table_sems, tile_sems = every_sem
    pieces = table_sems.shape[0]
    kinds = m2l_ref.shape[0]
    span = kinds // pieces
    received = recv_ref.shape[0]
    cells = acc.shape[0]
    leaves = rows_low.shape[0]
    entries = far_ref.shape[0] // leaves
    coarse, _ = coarse_from_ref.shape

    loads = [
        pltpu.make_async_copy(
            m2l_ref.at[k * span : (k + 1) * span], table.at[k * span : (k + 1) * span],
            table_sems.at[k],
        )
        for k in range(pieces)
    ]
    for load in loads:
        load.start()
    copies = load_window(begin, target_ref, [source_ref, after_ref], target, window, sems)
    groups_low[...] = jnp.zeros(groups_low.shape, F32)
    groups_high[...] = jnp.zeros(groups_high.shape, F32)
    acc[...] = jnp.zeros(acc.shape, F32)
    oct_size = parents_low.shape[0] // cells
    before = 0
    for part in parent_refs:
        for k in range(2):
            owner = lax.rem(lax.axis_index("oct") + oct_size - before, oct_size)
            at = pl.ds(pl.multiple_of(owner * cells, cells), cells)
            piece = part[k * 4 : k * 4 + 4].astype(F32)
            parents_low[at, :] = piece[0:2].reshape(cells, 128)
            parents_high[at, :] = piece[2:4].reshape(cells, 128)
            before += 1
    for k, part in enumerate(recv_refs):
        last = part.shape[0]
        recv_ref[k * 32 : (k + 1) * 32, :128] = part[last - 2]
        recv_ref[k * 32 : (k + 1) * 32, 128:] = part[last - 1]

    beside = 8

    def gather(block, carry):
        for j in range(coarse):
            loaded = []
            for u in range(beside):
                q = block * beside + u
                at = pl.ds(coarse_to_ref[j, q] * cells + q, 1)
                row = pl.ds(coarse_from_ref[j, q], 1)
                low = groups_low[at, :] + parents_low[row, :]
                high = groups_high[at, :] + parents_high[row, :]
                loaded.append((at, low, high))
            for at, low, high in loaded:
                groups_low[at, :] = low
                groups_high[at, :] = high
        return carry

    lax.fori_loop(0, cells // beside, gather, 0)
    tile_blocks, width = tile_ref.shape[0] // 32, 32
    slots = [kinds + width * k for k in range(tile_blocks - 3)] + [0, width, kinds]
    tiles = [
        pltpu.make_async_copy(
            tile_ref.at[k * width : (k + 1) * width], table.at[slots[k] : slots[k] + width],
            tile_sems.at[k],
        )
        for k in range(tile_blocks)
    ]
    for k in range(tile_blocks - 3):
        tiles[k].start()
    for k in range(pieces):
        loads[k].wait()

        def spread_out(t, carry):
            kind = k * span + t
            at = pl.ds(pl.multiple_of(kind * cells, cells), cells)
            group = jnp.concatenate([groups_low[at, :], groups_high[at, :]], axis=1).astype(BF)
            out = dot(recv_ref[...], table[kind])
            at = pl.ds(pl.multiple_of(kind * received, received), received)
            z[at, :] = out[:, :128]
            at = pl.ds(pl.multiple_of(second + kind * received, received // 2), received)
            z[at, :] = out[:, 128:]
            acc[...] += dot(group, table[kind])
            return carry

        lax.fori_loop(0, span, spread_out, 0, unroll=True)
    for k in range(tile_blocks - 3, tile_blocks - 1):
        tiles[k].start()
    local = acc[...].astype(BF)
    for c in range(8):
        out = dot(local, l2l_ref[c])
        at = received * kinds + c * cells
        z[pl.ds(at, cells), :] = out[:, :128]
        z[pl.ds(second + at, cells), :] = out[:, 128:]
    for copy in copies:
        copy.wait()
    per = leaves // target.shape[0]

    def body(group, carry):
        first = group * 64

        def add_rows(u):
            for v in range(per):
                leaf = first * per + u * per + v
                lows, highs = [None] * 4, [None] * 4
                for j in range(entries):
                    at = far_ref[j * leaves + leaf]
                    low, high = z[pl.ds(at, 1), :], z[pl.ds(second + at, 1), :]
                    k = j % 4
                    lows[k] = low if lows[k] is None else lows[k] + low
                    highs[k] = high if highs[k] is None else highs[k] + high
                at = pl.ds(leaf, 1)
                rows_low[at, :] = (lows[0] + lows[1]) + (lows[2] + lows[3])
                rows_high[at, :] = (highs[0] + highs[1]) + (highs[2] + highs[3])

        own = (offset_ref, dir_ref, scale_ref, add_ref, target, window, near_ref)
        near_leaves(begin, first, 64, own, add_rows)
        return carry

    lax.fori_loop(0, target.shape[0] // 64, body, 0)
    row = lax.broadcasted_iota(jnp.int32, (16, 128), 0)
    lane = lax.broadcasted_iota(jnp.int32, (16, 128), 1)
    for k in range(tile_blocks):
        tiles[k].wait()
        near_part = near_refs[k] if k < len(near_refs) else near_ref
        near_first = 0 if k < len(near_refs) else k * 2 * width - begin

        def far(group, carry):
            first = k * 2 * width + group * 16
            at = pl.ds(pl.multiple_of(first, 16), 16)
            local = jnp.concatenate([rows_low[at, :], rows_high[at, :]], axis=1).astype(BF)
            value = jnp.zeros((16, 128), F32)
            for u in range(8):
                out = dot(local, table[slots[k] + group * 8 + u])
                value = jnp.where(row == 2 * u, out[:, :128], value)
                value = jnp.where(row == 2 * u + 1, out[:, 128:], value)
            near = near_part[pl.ds(pl.multiple_of(near_first + group * 16, 16), 16), :]
            total = 0.5 * dens_ref[at, :] + near + value * (1.0 / math.sqrt(256))
            out_ref[at, :] = jnp.where(lane < spread(counts_ref, first, 16), total, 0.0)
            return carry

        lax.fori_loop(0, width // 8, far, 0, unroll=True)
        if k == 0:
            tiles[tile_blocks - 1].start()


def params(mib=56):
    return pltpu.CompilerParams(vmem_limit_bytes=mib * 2**20)


def local(
    density, positions, counts, leaf_parent, child_pos, send_slots, far_source, far_type,
    near_offset, near_dir, coarse_source, coarse_type, m2l, m2m, l2l,
):
    leaves, panels = density.shape
    width = m2l.shape[1]
    kinds = m2l.shape[0]
    cells = coarse_source.shape[0]
    oct_size, leaf_size = lax.axis_size("oct"), lax.axis_size("leaf")
    group, place = lax.axis_index("oct"), lax.axis_index("leaf")
    cap = send_slots.shape[2]
    planes = positions.transpose(1, 0, 2)
    checks = check_rows(width)
    scale, add = shift_rows()

    code = (child_pos * cells + leaf_parent)[None, :]

    steps = 8
    block = leaves // steps
    chunk = leaves // 8
    target, source, tile, *send = pl.pallas_call(
        functools.partial(moments_kernel, (oct_size, leaf_size)),
        grid=(steps,),
        in_specs=[
            SMEM, SMEM,
            pl.BlockSpec((3, block, panels), lambda i: (0, i, 0)),
            pl.BlockSpec((block, panels), lambda i: (i, 0)),
            VMEM, VMEM, VMEM,
        ],
        out_specs=[
            pl.BlockSpec((block, ROWS, panels), lambda i: (i, 0, 0)),
            pl.BlockSpec((block, ROWS, panels), lambda i: (i, 0, 0)),
            pl.BlockSpec((block // 2, width, 2 * panels), lambda i: (i, 0, 0)),
        ]
        + [VMEM] * 9,
        out_shape=[
            jax.ShapeDtypeStruct((leaves, ROWS, panels), BF),
            jax.ShapeDtypeStruct((leaves, ROWS, panels), BF),
            jax.ShapeDtypeStruct((leaves // 2, width, 2 * panels), BF),
        ]
        + [jax.ShapeDtypeStruct((n, 32, 128), BF) for n in (6, HW + 6, 2, HW + 2, 2, 2, 2, 2, 4)],
        scratch_shapes=[
            pltpu.VMEM((block, 128), F32),
            pltpu.VMEM((leaves, 128), F32),
            pltpu.VMEM((leaves, 128), F32),
            pltpu.VMEM((8 * PITCH, panels), F32),
            pltpu.VMEM((8 * PITCH, panels), F32),
        ],
        compiler_params=params(),
        name="moments",
    )(send_slots[0].T, counts, planes, density, code, checks.T, m2m)

    offsets = near_offset.T
    ways = near_dir.T

    spaces = [SMEM, SMEM, VMEM, VMEM, pl.BlockSpec(memory_space=pl.ANY)]

    def near_part(begin):
        parts = [before, source] if begin == 0 else [source]
        return pl.pallas_call(
            functools.partial(near_kernel, begin),
            in_specs=spaces + [pl.BlockSpec(memory_space=pl.ANY)] * len(parts),
            out_specs=VMEM,
            out_shape=jax.ShapeDtypeStruct((chunk, panels), F32),
            scratch_shapes=[
                pltpu.VMEM((chunk, ROWS, panels), BF),
                pltpu.VMEM((chunk + 2 * HW, ROWS, panels), BF),
                pltpu.SemaphoreType.DMA((3,)),
            ],
            compiler_params=params(),
            cost_estimate=pl.CostEstimate(
                flops=10**10, bytes_accessed=10**6, transcendentals=chunk * 2 * 65536
            ),
            name="near",
        )(offsets, ways, scale, add, target, *parts)

    def shifted(value, axis, by):
        size = lax.axis_size(axis)
        return lax.ppermute(value, axis, [(i, (i + by) % size) for i in range(size)])

    def added(pieces):
        total = pieces[0].astype(F32)
        for piece in pieces[1:]:
            total = total + piece.astype(F32)
        return total.astype(BF)

    partial = send[8]
    by_one = shifted(send[1], "leaf", 1)
    back_one = shifted(send[3], "leaf", -1)
    by_two = shifted(send[0], "leaf", 2)
    back_two = shifted(send[4], "leaf", -2)
    by_three = shifted(partial, "leaf", 3)
    near = [None] * 4
    near[1] = near_part(chunk)
    near[1], by_one, by_two, by_three, back_one, back_two = lax.optimization_barrier(
        (near[1], by_one, by_two, by_three, back_one, back_two)
    )
    before, after = by_one, back_one
    four = added([partial, by_one[HW : HW + 4], by_two[:4], by_three])
    strides = [shifted(four, "leaf", by) for by in (4, 8, 12)]
    upper = shifted(send[5], "oct", -1)
    four, source, target = lax.optimization_barrier((four, source, target))
    near[0] = near_part(0)
    near[0], four, upper, *strides = lax.optimization_barrier((near[0], four, upper, *strides))
    total = added([four, *strides])
    lower = shifted(jnp.concatenate([total, send[6]], axis=0), "oct", 1)
    total, source, target = lax.optimization_barrier((total, source, target))
    near[2] = near_part(2 * chunk)
    near[2], total, lower = lax.optimization_barrier((near[2], total, lower))
    pair = jnp.concatenate([total, lower[:4], send[7]], axis=0)
    pairs = [shifted(pair, "oct", by) for by in (2, 4, 6)]
    pair, source, target = lax.optimization_barrier((pair, source, target))
    near[3] = near_part(3 * chunk)
    near[3], pair, *pairs = lax.optimization_barrier((near[3], pair, *pairs))
    every_parent = [pair, *pairs]
    received = [by_two, by_one, send[2], back_one, back_two, upper, lower, pairs[1]]

    owner, slot = far_source // cap, far_source % cap
    owner_group, owner_place = owner // leaf_size, owner % leaf_size
    partner = jnp.where(
        owner_group == group,
        owner_place - place + 2,
        jnp.where(
            owner_group == (group + 1) % oct_size,
            5,
            jnp.where(owner_group == (group + oct_size - 1) % oct_size, 6, 7),
        ),
    )
    far_rows = (far_type * 8 + partner) * cap + slot
    own_row = kinds * 8 * cap + child_pos * cells + leaf_parent
    far_rows = jnp.concatenate([far_rows.T.reshape(-1), own_row])
    rest = leaves - 4 * chunk
    any_space = pl.BlockSpec(memory_space=pl.ANY)
    return pl.pallas_call(
        functools.partial(translate_kernel, 4 * chunk),
        in_specs=[SMEM] * 5 + [VMEM] * 3 + [any_space] * 4 + [VMEM] * 12
        + [SMEM, any_space] + [VMEM] * 5,
        out_specs=VMEM,
        out_shape=jax.ShapeDtypeStruct((leaves, panels), F32),
        scratch_shapes=[
            pltpu.VMEM((2 * (kinds * 8 * cap + 8 * cells), 128), F32),
            pltpu.VMEM((kinds * cells, 128), F32),
            pltpu.VMEM((kinds * cells, 128), F32),
            pltpu.VMEM((oct_size * cells, 128), F32),
            pltpu.VMEM((oct_size * cells, 128), F32),
            pltpu.VMEM((cells, width), F32),
            pltpu.VMEM((leaves, 128), F32),
            pltpu.VMEM((leaves, 128), F32),
            pltpu.VMEM((8 * cap, width), BF),
            pltpu.VMEM((rest, ROWS, panels), BF),
            pltpu.VMEM((rest + 2 * HW, ROWS, panels), BF),
            pltpu.VMEM((rest, panels), F32),
            pltpu.VMEM((kinds + 5 * 32, width, width), BF),
            pltpu.SemaphoreType.DMA((3,)),
            pltpu.SemaphoreType.DMA((8,)),
            pltpu.SemaphoreType.DMA((8,)),
        ],
        compiler_params=params(62),
        name="translate",
    )(
        offsets, ways, far_rows, coarse_source.T, coarse_type.T, scale, add, l2l,
        target, source, after, m2l, *received, *every_parent, counts, tile, density, *near,
    )


def solution(mesh):
    both = ("oct", "leaf")
    placed = (
        P(both, None), P(both, None, None), P(both), P(both), P(both), P(both, None, None),
        P(both, None), P(both, None), P(both, None), P(both, None),
        P("oct", None), P("oct", None), P(), P(), P(),
    )
    return jax.shard_map(
        local, mesh=mesh, in_specs=placed, out_specs=P(both, None), check_vma=False
    )
```

```python
import functools
import math

import jax
import jax.numpy as jnp
import ml_dtypes
import numpy as np
from jax import lax
from jax.experimental import pallas as pl
from jax.experimental.pallas import tpu as pltpu
from jax.sharding import PartitionSpec as P

HW = 32
KAPPA = 0.25
DELTA = 0.05
RADIUS = 2.0
RATE = -KAPPA * math.log2(math.e)
ROWS = 32
PITCH = 36
BF = jnp.bfloat16
F32 = jnp.float32
VMEM = pl.BlockSpec(memory_space=pltpu.VMEM)
SMEM = pl.BlockSpec(memory_space=pltpu.SMEM)


def np_split(values, number):
    pieces = []
    rest = values.astype(np.float32)
    for _ in range(number):
        piece = rest.astype(ml_dtypes.bfloat16)
        pieces.append(piece)
        rest = rest - piece.astype(np.float32)
    return pieces


def check_rows(number):
    middle = np.arange(number, dtype=np.float32) + np.float32(0.5)
    height = (1.0 - 2.0 * middle / np.float32(number)).astype(np.float32)
    radial = np.sqrt(np.maximum(1.0 - height * height, 0.0)).astype(np.float32)
    azimuth = np.float32(math.pi * (1.0 + math.sqrt(5.0))) * middle
    points = RADIUS * np.stack([radial * np.cos(azimuth), radial * np.sin(azimuth), height])
    high, low = np_split(points, 2)
    high, low = high.astype(np.float32), low.astype(np.float32)
    rounded = high + low
    squares = np_split(np.sum(rounded * rounded, axis=0), 3)
    rows = np.zeros((ROWS, number), np.float32)
    rows[0:3], rows[3:6], rows[6:9], rows[9:12] = -2 * high, -2 * low, -2 * high, -2 * low
    for k in range(3):
        rows[12 + k] = squares[k].astype(np.float32)
    rows[15:18] = 1.0
    return rows.astype(ml_dtypes.bfloat16)


def shift_rows():
    scale = np.zeros((27, ROWS, 128), np.float32)
    add = np.zeros((27, ROWS, 128), np.float32)
    scale[:, 0:18] = 1.0
    scale[:, 31] = 1.0
    for d in range(27):
        shift = 2.0 * np.array([d // 9 - 1, d // 3 % 3 - 1, d % 3 - 1], np.float32)
        for k in range(3):
            scale[d, 18 + k] = -shift[k]
            scale[d, 21 + k] = -shift[k]
            add[d, 24 + k] = -2 * shift[k]
            add[d, 27 + k] = -2 * shift[k]
        add[d, 30] = np.sum(shift * shift)
    return scale.astype(ml_dtypes.bfloat16), add.astype(ml_dtypes.bfloat16)


def split(value):
    high = value.astype(BF).astype(F32)
    return high, value - high


def panel_rows(coords, weights):
    highs, lows, square = [], [], None
    for value in coords:
        high, rest = split(value)
        low = rest.astype(BF).astype(F32)
        highs.append(high)
        lows.append(low)
        rounded = high + low
        square = rounded * rounded if square is None else square + rounded * rounded
    one = jnp.ones_like(square)
    zero = jnp.zeros_like(square)

    def thirds(value):
        first, rest = split(value)
        second, rest = split(rest)
        return [first, second, rest]

    minus_high = [-2.0 * value for value in highs]
    minus_low = [-2.0 * value for value in lows]
    target = highs + highs + lows + lows + [one] * 3 + thirds(square + DELTA * DELTA)
    target += [one] * 6 + highs + lows + [one, zero]
    source = minus_high + minus_low + minus_high + minus_low + thirds(square) + [one] * 3
    source += minus_high + minus_low + [zero] * 7 + [weights]
    return target, source


def spread(ref, first, number):
    row = lax.broadcasted_iota(jnp.int32, (number, 128), 0)
    value = jnp.full((number, 128), ref[first], jnp.int32)
    for u in range(1, number):
        value = jnp.where(row == u, ref[first + u], value)
    return value


def place_rows(rows, scratch, write):
    for r, value in enumerate(rows):
        scratch[pl.ds(r, 8, stride=PITCH), :] = value
    for u in range(8):
        write(u, scratch[u * PITCH : u * PITCH + ROWS, :].astype(BF))


def green(squared):
    low = squared.astype(BF)
    inverse = lax.rsqrt(low)
    return jnp.exp2((low * inverse) * BF(RATE)) * inverse


def dot(a, b, over=((1,), (0,))):
    return lax.dot_general(a, b, (over, ((), ())), preferred_element_type=F32)


def moments_kernel(
    sizes, slots_ref, counts_ref, pos_ref, dens_ref, code_ref, checks_ref, m2m_ref,
    target_ref, source_ref, tile_ref, *rest,
):
    send_refs, part_refs = rest[:8], ((rest[8], 0), (rest[0], 0), (rest[1], HW))
    weights, moments_low, moments_high, scratch, spare = rest[9:]
    step = pl.program_id(0)
    leaves = pos_ref.shape[1]
    total = moments_low.shape[0]
    checks = checks_ref[...]
    lane = lax.broadcasted_iota(jnp.int32, (8, 128), 1)

    def build(group, carry):
        at = pl.ds(pl.multiple_of(group * 8, 8), 8)
        masked = jnp.where(lane < spread(counts_ref, step * leaves + group * 8, 8), dens_ref[at, :], 0.0)
        weights[at, :] = masked
        target, source = panel_rows([pos_ref[d, at, :] for d in range(3)], masked)

        def put_target(u, value):
            target_ref[group * 8 + u] = value

        def put_source(u, value):
            source_ref[group * 8 + u] = value

        place_rows(target, scratch, put_target)
        place_rows(source, spare, put_source)
        return carry

    lax.fori_loop(0, leaves // 8, build, 0)
    row = lax.broadcasted_iota(jnp.int32, (16, 128), 0)

    def squares(leaf):
        return dot(checks, jnp.concatenate([target_ref[leaf + u] for u in range(2)], axis=1))

    def finish(first, part, kernel, sums):
        tile_ref[first // 2 + part] = kernel
        block = part // 8
        value = weights[pl.ds(pl.multiple_of(first + block * 16, 16), 16), :]
        apart = [jnp.where(row == part % 8 * 2 + u, value, 0.0) for u in range(2)]
        out = dot(jnp.concatenate(apart, axis=1).astype(BF), kernel, ((1,), (1,)))
        sums[block] = out if part % 8 == 0 else sums[block] + out
        if part % 8 == 7:
            low = (sums[block] * (1.0 / math.sqrt(128))).astype(BF).astype(F32)
            at = pl.ds(pl.multiple_of(step * leaves + first + block * 16, 16), 16)
            moments_low[at, :], moments_high[at, :] = low[:, :128], low[:, 128:]

    def expand(group, carry):
        first = group * span
        ahead, kernels, sums = {}, {}, {}
        for s in range(span // 2 + 4):
            if s < span // 2:
                ahead[s] = squares(first + s * 2)
            if 0 <= s - 2 < span // 2:
                kernels[s - 2] = green(ahead.pop(s - 2))
            if 0 <= s - 4:
                finish(first, s - 4, kernels.pop(s - 4), sums)
        return carry

    span = 64
    lax.fori_loop(0, leaves // span, expand, 0)

    @pl.when(step == 0)
    def _():
        send_refs[3][0:HW] = source_ref[0:HW]

    @pl.when(step == pl.num_programs(0) - 1)
    def _():
        send_refs[1][0:HW] = source_ref[leaves - HW :]
        group, place = lax.axis_index("oct"), lax.axis_index("leaf")
        oct_size, leaf_size = sizes
        for partner in range(8):
            if partner < 5:
                other = jnp.clip(place + 2 - partner, 0, leaf_size - 1)
                other = group * leaf_size + other
            else:
                by = (oct_size - 1, 1, oct_size // 2)[partner - 5]
                other = lax.rem(group + by, oct_size) * leaf_size + place

            def pick(s, carry):
                slot = jnp.maximum(slots_ref[s, other], 0)
                spare[pl.ds(s, 1), :] = moments_low[pl.ds(slot, 1), :]
                scratch[pl.ds(s, 1), :] = moments_high[pl.ds(slot, 1), :]
                return carry

            lax.fori_loop(0, 32, pick, 0, unroll=8)
            last = send_refs[partner].shape[0]
            send_refs[partner][last - 2] = spare[0:32, :].astype(BF)
            send_refs[partner][last - 1] = scratch[0:32, :].astype(BF)
        low = jnp.concatenate([moments_low[...], moments_high[...]], axis=1).astype(BF)
        parents = 64
        acc = jnp.zeros((parents, 2 * 128), F32)
        for c in range(8):
            row = lax.broadcasted_iota(jnp.int32, (parents, total), 0) + c * parents
            chosen = jnp.where(row == code_ref[...], 1.0, 0.0).astype(BF)
            high, rest = split(dot(chosen, low))
            acc += dot(high.astype(BF), m2m_ref[c]) + dot(rest.astype(BF), m2m_ref[c])
        for part_ref, at in part_refs:
            for k in range(4):
                piece = acc[k % 2 * 32 : k % 2 * 32 + 32, k // 2 * 128 : k // 2 * 128 + 128]
                part_ref[at + k] = piece.astype(BF)


def load_window(begin, target_ref, parts, target, window, sems):
    leaves = target.shape[0]
    copies = [pltpu.make_async_copy(target_ref.at[begin : begin + leaves], target, sems.at[2])]
    at = 0
    for k, part in enumerate(parts):
        size = part.shape[0]
        if size < 64:
            size, part = HW, part.at[0:HW]
        if part.shape[0] >= 64:
            low = max(begin - HW, 0)
            size = min(begin + leaves + HW, size) - low
            part = part.at[low : low + size]
        copies.append(pltpu.make_async_copy(part, window.at[at : at + size], sems.at[k]))
        at += size
    for copy in copies:
        copy.start()
    return copies


def near_leaves(begin, first, number, refs, beside=None):
    offset_ref, dir_ref, scale_ref, add_ref, target, window, out_ref = refs

    def squares(leaf):
        whole = begin + leaf
        rows, weights = [], []
        for j in range(4):
            base = window[leaf + HW + offset_ref[j, whole]]
            way = dir_ref[j, whole]
            rows.append(base * scale_ref[way] + add_ref[way])
            weights.append(base[16:32])
        value = dot(target[leaf], jnp.concatenate(rows, 1), ((0,), (0,)))
        return value, jnp.concatenate(weights, 1)

    depth = 2
    ahead = []
    for u in range(number + depth):
        if u < number:
            ahead.append(squares(first + u))
            if beside is not None:
                beside(u)
        if u >= depth:
            value, weights = ahead[u - depth]
            ahead[u - depth] = None
            out = dot(weights, green(value), ((1,), (1,)))[15:16]
            out_ref[pl.ds(first + u - depth, 1), :] = out * (1.0 / math.sqrt(512))


def near_kernel(begin, offset_ref, dir_ref, scale_ref, add_ref, target_ref, *refs):
    *parts, out_ref, target, window, sems = refs
    for copy in load_window(begin, target_ref, parts, target, window, sems):
        copy.wait()

    def body(group, carry):
        own = (offset_ref, dir_ref, scale_ref, add_ref, target, window, out_ref)
        near_leaves(begin, group * 32, 32, own)
        return carry

    lax.fori_loop(0, target.shape[0] // 32, body, 0)


def translate_kernel(
    begin, offset_ref, dir_ref, far_ref, coarse_from_ref, coarse_to_ref,
    scale_ref, add_ref, l2l_ref, target_ref, source_ref, after_ref, m2l_ref, *refs,
):
    recv_refs, parent_refs = refs[:8], refs[8:12]
    counts_ref, tile_ref, dens_ref, *near_refs, out_ref = refs[12:20]
    z, groups_low, groups_high, parents_low, parents_high = refs[20:25]
    acc, rows_low, rows_high, recv_ref, target, window, near_ref, table, *every_sem = refs[25:]
    second = z.shape[0] // 2
    sems, table_sems, tile_sems = every_sem
    pieces = table_sems.shape[0]
    kinds = m2l_ref.shape[0]
    span = kinds // pieces
    received = recv_ref.shape[0]
    cells = acc.shape[0]
    leaves = rows_low.shape[0]
    entries = far_ref.shape[0] // leaves
    coarse, _ = coarse_from_ref.shape

    loads = [
        pltpu.make_async_copy(
            m2l_ref.at[k * span : (k + 1) * span], table.at[k * span : (k + 1) * span],
            table_sems.at[k],
        )
        for k in range(pieces)
    ]
    for load in loads:
        load.start()
    copies = load_window(begin, target_ref, [source_ref, after_ref], target, window, sems)
    groups_low[...] = jnp.zeros(groups_low.shape, F32)
    groups_high[...] = jnp.zeros(groups_high.shape, F32)
    acc[...] = jnp.zeros(acc.shape, F32)
    oct_size = parents_low.shape[0] // cells
    before = 0
    for part in parent_refs:
        for k in range(2):
            owner = lax.rem(lax.axis_index("oct") + oct_size - before, oct_size)
            at = pl.ds(pl.multiple_of(owner * cells, cells), cells)
            piece = part[k * 4 : k * 4 + 4].astype(F32)
            parents_low[at, :] = piece[0:2].reshape(cells, 128)
            parents_high[at, :] = piece[2:4].reshape(cells, 128)
            before += 1
    for k, part in enumerate(recv_refs):
        last = part.shape[0]
        recv_ref[k * 32 : (k + 1) * 32, :128] = part[last - 2]
        recv_ref[k * 32 : (k + 1) * 32, 128:] = part[last - 1]

    beside = 8

    def gather(block, carry):
        for j in range(coarse):
            loaded = []
            for u in range(beside):
                q = block * beside + u
                at = pl.ds(coarse_to_ref[j, q] * cells + q, 1)
                row = pl.ds(coarse_from_ref[j, q], 1)
                low = groups_low[at, :] + parents_low[row, :]
                high = groups_high[at, :] + parents_high[row, :]
                loaded.append((at, low, high))
            for at, low, high in loaded:
                groups_low[at, :] = low
                groups_high[at, :] = high
        return carry

    lax.fori_loop(0, cells // beside, gather, 0)
    tile_blocks, width = tile_ref.shape[0] // 32, 32
    slots = [kinds + width * k for k in range(tile_blocks - 3)] + [0, width, kinds]
    tiles = [
        pltpu.make_async_copy(
            tile_ref.at[k * width : (k + 1) * width], table.at[slots[k] : slots[k] + width],
            tile_sems.at[k],
        )
        for k in range(tile_blocks)
    ]
    for k in range(tile_blocks - 3):
        tiles[k].start()
    for k in range(pieces):
        loads[k].wait()

        def spread_out(t, carry):
            kind = k * span + t
            at = pl.ds(pl.multiple_of(kind * cells, cells), cells)
            group = jnp.concatenate([groups_low[at, :], groups_high[at, :]], axis=1).astype(BF)
            out = dot(recv_ref[...], table[kind])
            at = pl.ds(pl.multiple_of(kind * received, received), received)
            z[at, :] = out[:, :128]
            at = pl.ds(pl.multiple_of(second + kind * received, received // 2), received)
            z[at, :] = out[:, 128:]
            acc[...] += dot(group, table[kind])
            return carry

        lax.fori_loop(0, span, spread_out, 0, unroll=True)
    for k in range(tile_blocks - 3, tile_blocks - 1):
        tiles[k].start()
    local = acc[...].astype(BF)
    for c in range(8):
        out = dot(local, l2l_ref[c])
        at = received * kinds + c * cells
        z[pl.ds(at, cells), :] = out[:, :128]
        z[pl.ds(second + at, cells), :] = out[:, 128:]
    for copy in copies:
        copy.wait()
    per = leaves // target.shape[0]

    def body(group, carry):
        first = group * 32

        def add_rows(u):
            for v in range(per):
                leaf = first * per + u * per + v
                lows, highs = [None] * 4, [None] * 4
                for j in range(entries):
                    at = far_ref[j * leaves + leaf]
                    low, high = z[pl.ds(at, 1), :], z[pl.ds(second + at, 1), :]
                    k = j % 4
                    lows[k] = low if lows[k] is None else lows[k] + low
                    highs[k] = high if highs[k] is None else highs[k] + high
                at = pl.ds(leaf, 1)
                rows_low[at, :] = (lows[0] + lows[1]) + (lows[2] + lows[3])
                rows_high[at, :] = (highs[0] + highs[1]) + (highs[2] + highs[3])

        own = (offset_ref, dir_ref, scale_ref, add_ref, target, window, near_ref)
        near_leaves(begin, first, 32, own, add_rows)
        return carry

    lax.fori_loop(0, target.shape[0] // 32, body, 0)
    row = lax.broadcasted_iota(jnp.int32, (16, 128), 0)
    lane = lax.broadcasted_iota(jnp.int32, (16, 128), 1)
    for k in range(tile_blocks):
        tiles[k].wait()
        near_part = near_refs[k] if k < len(near_refs) else near_ref
        near_first = 0 if k < len(near_refs) else k * 2 * width - begin

        def far(group, carry):
            first = k * 2 * width + group * 16
            at = pl.ds(pl.multiple_of(first, 16), 16)
            local = jnp.concatenate([rows_low[at, :], rows_high[at, :]], axis=1).astype(BF)
            value = jnp.zeros((16, 128), F32)
            for u in range(8):
                out = dot(local, table[slots[k] + group * 8 + u])
                value = jnp.where(row == 2 * u, out[:, :128], value)
                value = jnp.where(row == 2 * u + 1, out[:, 128:], value)
            near = near_part[pl.ds(pl.multiple_of(near_first + group * 16, 16), 16), :]
            total = 0.5 * dens_ref[at, :] + near + value * (1.0 / math.sqrt(256))
            out_ref[at, :] = jnp.where(lane < spread(counts_ref, first, 16), total, 0.0)
            return carry

        lax.fori_loop(0, width // 8, far, 0, unroll=True)
        if k == 0:
            tiles[tile_blocks - 1].start()


def params(mib=56):
    return pltpu.CompilerParams(vmem_limit_bytes=mib * 2**20)


def local(
    density, positions, counts, leaf_parent, child_pos, send_slots, far_source, far_type,
    near_offset, near_dir, coarse_source, coarse_type, m2l, m2m, l2l,
):
    leaves, panels = density.shape
    width = m2l.shape[1]
    kinds = m2l.shape[0]
    cells = coarse_source.shape[0]
    oct_size, leaf_size = lax.axis_size("oct"), lax.axis_size("leaf")
    group, place = lax.axis_index("oct"), lax.axis_index("leaf")
    cap = send_slots.shape[2]
    planes = positions.transpose(1, 0, 2)
    checks = check_rows(width)
    scale, add = shift_rows()

    code = (child_pos * cells + leaf_parent)[None, :]

    steps = 8
    block = leaves // steps
    chunk = leaves // 8
    target, source, tile, *send = pl.pallas_call(
        functools.partial(moments_kernel, (oct_size, leaf_size)),
        grid=(steps,),
        in_specs=[
            SMEM, SMEM,
            pl.BlockSpec((3, block, panels), lambda i: (0, i, 0)),
            pl.BlockSpec((block, panels), lambda i: (i, 0)),
            VMEM, VMEM, VMEM,
        ],
        out_specs=[
            pl.BlockSpec((block, ROWS, panels), lambda i: (i, 0, 0)),
            pl.BlockSpec((block, ROWS, panels), lambda i: (i, 0, 0)),
            pl.BlockSpec((block // 2, width, 2 * panels), lambda i: (i, 0, 0)),
        ]
        + [VMEM] * 9,
        out_shape=[
            jax.ShapeDtypeStruct((leaves, ROWS, panels), BF),
            jax.ShapeDtypeStruct((leaves, ROWS, panels), BF),
            jax.ShapeDtypeStruct((leaves // 2, width, 2 * panels), BF),
        ]
        + [jax.ShapeDtypeStruct((n, 32, 128), BF) for n in (6, HW + 6, 2, HW + 2, 2, 2, 2, 2, 4)],
        scratch_shapes=[
            pltpu.VMEM((block, 128), F32),
            pltpu.VMEM((leaves, 128), F32),
            pltpu.VMEM((leaves, 128), F32),
            pltpu.VMEM((8 * PITCH, panels), F32),
            pltpu.VMEM((8 * PITCH, panels), F32),
        ],
        compiler_params=params(),
        name="moments",
    )(send_slots[0].T, counts, planes, density, code, checks.T, m2m)

    offsets = near_offset.T
    ways = near_dir.T

    spaces = [SMEM, SMEM, VMEM, VMEM, pl.BlockSpec(memory_space=pl.ANY)]

    def near_part(begin):
        parts = [before, source] if begin == 0 else [source]
        return pl.pallas_call(
            functools.partial(near_kernel, begin),
            in_specs=spaces + [pl.BlockSpec(memory_space=pl.ANY)] * len(parts),
            out_specs=VMEM,
            out_shape=jax.ShapeDtypeStruct((chunk, panels), F32),
            scratch_shapes=[
                pltpu.VMEM((chunk, ROWS, panels), BF),
                pltpu.VMEM((chunk + 2 * HW, ROWS, panels), BF),
                pltpu.SemaphoreType.DMA((3,)),
            ],
            compiler_params=params(),
            cost_estimate=pl.CostEstimate(
                flops=10**10, bytes_accessed=10**6, transcendentals=chunk * 2 * 65536
            ),
            name="near",
        )(offsets, ways, scale, add, target, *parts)

    def shifted(value, axis, by):
        size = lax.axis_size(axis)
        return lax.ppermute(value, axis, [(i, (i + by) % size) for i in range(size)])

    def added(pieces):
        total = pieces[0].astype(F32)
        for piece in pieces[1:]:
            total = total + piece.astype(F32)
        return total.astype(BF)

    partial = send[8]
    by_one = shifted(send[1], "leaf", 1)
    back_one = shifted(send[3], "leaf", -1)
    by_two = shifted(send[0], "leaf", 2)
    back_two = shifted(send[4], "leaf", -2)
    by_three = shifted(partial, "leaf", 3)
    near = [None] * 4
    near[1] = near_part(chunk)
    near[1], by_one, by_two, by_three, back_one, back_two = lax.optimization_barrier(
        (near[1], by_one, by_two, by_three, back_one, back_two)
    )
    before, after = by_one, back_one
    four = added([partial, by_one[HW : HW + 4], by_two[:4], by_three])
    strides = [shifted(four, "leaf", by) for by in (4, 8, 12)]
    upper = shifted(send[5], "oct", -1)
    four, source, target = lax.optimization_barrier((four, source, target))
    near[0] = near_part(0)
    near[0], four, upper, *strides = lax.optimization_barrier((near[0], four, upper, *strides))
    total = added([four, *strides])
    lower = shifted(jnp.concatenate([total, send[6]], axis=0), "oct", 1)
    total, source, target = lax.optimization_barrier((total, source, target))
    near[2] = near_part(2 * chunk)
    near[2], total, lower = lax.optimization_barrier((near[2], total, lower))
    pair = jnp.concatenate([total, lower[:4], send[7]], axis=0)
    pairs = [shifted(pair, "oct", by) for by in (2, 4, 6)]
    pair, source, target = lax.optimization_barrier((pair, source, target))
    near[3] = near_part(3 * chunk)
    near[3], pair, *pairs = lax.optimization_barrier((near[3], pair, *pairs))
    every_parent = [pair, *pairs]
    received = [by_two, by_one, send[2], back_one, back_two, upper, lower, pairs[1]]

    owner, slot = far_source // cap, far_source % cap
    owner_group, owner_place = owner // leaf_size, owner % leaf_size
    partner = jnp.where(
        owner_group == group,
        owner_place - place + 2,
        jnp.where(
            owner_group == (group + 1) % oct_size,
            5,
            jnp.where(owner_group == (group + oct_size - 1) % oct_size, 6, 7),
        ),
    )
    far_rows = (far_type * 8 + partner) * cap + slot
    own_row = kinds * 8 * cap + child_pos * cells + leaf_parent
    far_rows = jnp.concatenate([far_rows.T.reshape(-1), own_row])
    rest = leaves - 4 * chunk
    any_space = pl.BlockSpec(memory_space=pl.ANY)
    return pl.pallas_call(
        functools.partial(translate_kernel, 4 * chunk),
        in_specs=[SMEM] * 5 + [VMEM] * 3 + [any_space] * 4 + [VMEM] * 12
        + [SMEM, any_space] + [VMEM] * 5,
        out_specs=VMEM,
        out_shape=jax.ShapeDtypeStruct((leaves, panels), F32),
        scratch_shapes=[
            pltpu.VMEM((2 * (kinds * 8 * cap + 8 * cells), 128), F32),
            pltpu.VMEM((kinds * cells, 128), F32),
            pltpu.VMEM((kinds * cells, 128), F32),
            pltpu.VMEM((oct_size * cells, 128), F32),
            pltpu.VMEM((oct_size * cells, 128), F32),
            pltpu.VMEM((cells, width), F32),
            pltpu.VMEM((leaves, 128), F32),
            pltpu.VMEM((leaves, 128), F32),
            pltpu.VMEM((8 * cap, width), BF),
            pltpu.VMEM((rest, ROWS, panels), BF),
            pltpu.VMEM((rest + 2 * HW, ROWS, panels), BF),
            pltpu.VMEM((rest, panels), F32),
            pltpu.VMEM((kinds + 5 * 32, width, width), BF),
            pltpu.SemaphoreType.DMA((3,)),
            pltpu.SemaphoreType.DMA((8,)),
            pltpu.SemaphoreType.DMA((8,)),
        ],
        compiler_params=params(62),
        name="translate",
    )(
        offsets, ways, far_rows, coarse_source.T, coarse_type.T, scale, add, l2l,
        target, source, after, m2l, *received, *every_parent, counts, tile, density, *near,
    )


def solution(mesh):
    both = ("oct", "leaf")
    placed = (
        P(both, None), P(both, None, None), P(both), P(both), P(both), P(both, None, None),
        P(both, None), P(both, None), P(both, None), P(both, None),
        P("oct", None), P("oct", None), P(), P(), P(),
    )
    return jax.shard_map(
        local, mesh=mesh, in_specs=placed, out_specs=P(both, None), check_vma=False
    )
```
